256 devices in a mesh: lat: 32 (over x_lo, z, core), lev: 8 (over y, x_hi).
Axes of the slice: x: 4 (x_hi: 2, x_lo: 2; x = x_hi * 2 + x_lo), y: 4, z: 8, core: 2. Of those that a mesh axis runs over, the one named last changes fastest.
Arguments:
- adjoint_in: float32 [64, 512, 1440], P('lev', 'lat'), may hold values from -6 to 6
- courant_lon: float32 [64, 512, 1440], P('lev', 'lat'), may hold values from -0.9 to 0.9
- codes_lon: int32 [64, 512, 1440], P('lev', 'lat'), may hold values from 0 to 3
- courant_lat: float32 [64, 512, 1440], P('lev', 'lat'), may hold values from -0.9 to 0.9
- codes_lat: int32 [64, 512, 1440], P('lev', 'lat'), may hold values from 0 to 3
- courant_lev: float32 [64, 512, 1440], P(None, 'lat', 'lev'), may hold values from -0.9 to 0.9
- codes_lev: int32 [64, 512, 1440], P(None, 'lat', 'lev'), may hold values from 0 to 3
- block_inverse: float32 [512, 4, 16, 16], P('lat'), may hold values from -1 to 1.5
- block_lower: float32 [512, 3, 16, 16], P('lat'), may hold values from -0.6 to 0.6
- block_upper: float32 [512, 3, 16, 16], P('lat'), may hold values from -0.6 to 0.6
- region_ids: int32 [512, 1440], P('lat'), may hold values from 0 to 1999
- owner: int32 [2000], replicated, may hold values from 0 to 255, as said below
Outputs:
- adjoint_out: float32 [64, 512, 1440], P('lev', 'lat')
- region_sens: float32 [4096, 64], P(('lat', 'lev'))
The draws below stay inside these ranges and needn't reach their ends.
Inputs may be any that keep to these rules, and one draw needn't show every extreme that they name: owner is a device index along lat+lev (lat slowest); no device owns more than 16 regions, and some device owns exactly 16.
All inputs are finite; a program needn't handle non-finite values.
Results may differ from the reference program's by a relative error of at most 0.0003.
Values sent between devices are 32-bit elements; how exact they have to be, the bound alone decides.
No kernel may reach another device: no remote copies, remote signals or barrier semaphores. Data moves between devices by JAX's collectives and lax.ppermute only.
A program may use at most 64 MiB of HBM per device.

```python
import jax
import jax.numpy as jnp
from jax import lax

NLON = 1440
NLEV = 64
BLOCK = 16
SUB = 2
NREG = 2000
NLAT = 512
NB = 4
REG_MOST = 16
N_LAT = 32
N_LEV = 8


def draw_block_inverse(key, part):
    key = jax.random.fold_in(key, 11)
    diag_key, off_key = jax.random.split(key)
    full_shape = (NLAT, NLEV // BLOCK, BLOCK, BLOCK)
    diagonal = jax.random.uniform(diag_key, full_shape[:3], jnp.float32, 0.6, 1.0)
    spread = jnp.clip(0.06 * jax.random.normal(off_key, full_shape, jnp.float32), -0.3, 0.3)
    identity = jnp.eye(BLOCK, dtype=jnp.float32)
    return diagonal[..., None] * identity + spread


def draw_owner(key, part):
    key = jax.random.fold_in(key, 23)
    pick_key, shuffle_key = jax.random.split(key)
    capacity = REG_MOST
    slot_total = N_LAT * N_LEV * capacity
    chosen = jax.random.randint(pick_key, (), 0, N_LAT * N_LEV)
    slot_index = jnp.arange(slot_total, dtype=jnp.int32)
    shuffled = jax.random.permutation(shuffle_key, slot_total).astype(jnp.int32)
    ranking = jnp.where(slot_index // capacity == chosen, slot_index - slot_total, shuffled)
    picked = jnp.argsort(ranking, stable=True)[:NREG]
    return (picked // capacity).astype(jnp.int32)


def place_ends(result, stream_key, smallest, largest):
    place = [jax.random.randint(jax.random.fold_in(stream_key, axis), (), 0, length) for axis, length in enumerate(result.shape)]
    widest = result.shape.index(max(result.shape))
    beside = place[:widest] + [(place[widest] + 1) % result.shape[widest]] + place[widest + 1:]
    return result.at[tuple(place)].set(smallest).at[tuple(beside)].set(largest)


def level_of(stream_key, shape, cuts, smallest, largest):
    def one(position, parts):
        steps = jax.random.uniform(jax.random.fold_in(jax.random.fold_in(stream_key, 6), position), (parts,), jnp.float32, smallest / len(cuts), largest / len(cuts))
        return jnp.repeat(jnp.exp(steps), shape[position] // parts).reshape((-1,) + (1,) * (len(shape) - position - 1))

    factor_of = one(*cuts[0])
    for cut in cuts[1:]:
        factor_of = factor_of * one(*cut)
    return factor_of


def centred(stream_key, dims, scale, reach, shards=(), kind=jnp.bfloat16):
    loudness = level_of(stream_key, dims, shards, -0.22, 0.18) if shards else 1.0
    entries = jax.random.normal(stream_key, dims, jnp.float32) * scale * loudness
    return jnp.minimum(jnp.maximum(entries, -reach), reach).astype(kind)


def setup_inputs(seed: int = 0) -> dict:
    keys = jax.random.split(jax.random.key(seed), 13)
    return {
        "adjoint_in": centred(keys[0], (NLEV, NLAT, NLON), 1.0, 6.0, ((0, 8), (1, 32)), jnp.float32),
        "courant_lon": jnp.clip(jax.random.uniform(keys[1], (NLEV, NLAT, NLON), jnp.float32, -0.9, 0.9) * level_of(keys[1], (NLEV, NLAT, NLON), ((0, 8), (1, 32)), -0.4, 0.0), -0.9, 0.9),
        "codes_lon": place_ends(jax.random.randint(keys[2], (NLEV, NLAT, NLON), 0, 4), jax.random.fold_in(keys[2], 1), 0, 3).astype(jnp.int32),
        "courant_lat": jnp.clip(jax.random.uniform(keys[3], (NLEV, NLAT, NLON), jnp.float32, -0.9, 0.9) * level_of(keys[3], (NLEV, NLAT, NLON), ((0, 8), (1, 32)), -0.4, 0.0), -0.9, 0.9),
        "codes_lat": place_ends(jax.random.randint(keys[4], (NLEV, NLAT, NLON), 0, 4), jax.random.fold_in(keys[4], 1), 0, 3).astype(jnp.int32),
        "courant_lev": jnp.clip(jax.random.uniform(keys[5], (NLEV, NLAT, NLON), jnp.float32, -0.9, 0.9) * level_of(keys[5], (NLEV, NLAT, NLON), ((1, 32), (2, 8)), -0.4, 0.0), -0.9, 0.9),
        "codes_lev": place_ends(jax.random.randint(keys[6], (NLEV, NLAT, NLON), 0, 4), jax.random.fold_in(keys[6], 1), 0, 3).astype(jnp.int32),
        "block_inverse": draw_block_inverse(jax.random.fold_in(keys[12], 71), 0),
        "block_lower": centred(keys[8], (NLAT, NB - 1, BLOCK, BLOCK), 0.1, 0.6, ((0, 32),), jnp.float32),
        "block_upper": centred(keys[9], (NLAT, NB - 1, BLOCK, BLOCK), 0.1, 0.6, ((0, 32),), jnp.float32),
        "region_ids": place_ends(jax.random.randint(keys[10], (NLAT, NLON), 0, NREG), jax.random.fold_in(keys[10], 1), 0, NREG - 1).astype(jnp.int32),
        "owner": draw_owner(jax.random.fold_in(keys[12], 71), 0),
    }


def pad_along(array, before_cells, after_cells, along, pad_mode):
    widths = [(0, 0)] * array.ndim
    widths[along] = (before_cells, after_cells)
    return jnp.pad(array, widths, mode=pad_mode)

def sweep_core(tracer, courant, codes, along):
    length = tracer.shape[along]

    def window(array, first_cell, end_cell):
        return lax.slice_in_dim(array, first_cell, end_cell, axis=along)
    centre = window(tracer, 1, length - 1)
    next_cell = window(tracer, 2, length)
    behind = window(tracer, 0, length - 2)
    slopes = jnp.where(codes == 1, next_cell - centre, jnp.where(codes == 2, centre - behind, jnp.where(codes == 3, 0.5 * (next_cell - behind), 0.0)))
    low_cell = window(tracer, 1, length - 2)
    up_cell = window(tracer, 2, length - 1)
    low_slope = window(slopes, 0, length - 3)
    up_slope = window(slopes, 1, length - 2)
    fluxes = jnp.maximum(courant, 0.0) * (low_cell + 0.5 * (1.0 - courant) * low_slope) + jnp.minimum(courant, 0.0) * (up_cell - 0.5 * (1.0 + courant) * up_slope)
    return window(tracer, 2, length - 2) - (window(fluxes, 1, length - 3) - window(fluxes, 0, length - 4))

def wall_forward(tracer, courant, codes, along):
    length = tracer.shape[along]
    inside = lax.broadcasted_iota(jnp.int32, courant.shape, along) < length - 1
    walled = jnp.where(inside, courant, 0.0)
    return sweep_core(pad_along(tracer, 2, 2, along, 'constant'), pad_along(walled, 1, 0, along, 'constant'), pad_along(codes, 1, 1, along, 'constant'), along)

def cycle_forward(tracer, courant, codes, along):
    return sweep_core(pad_along(tracer, 2, 2, along, 'wrap'), pad_along(courant, 1, 0, along, 'wrap'), pad_along(codes, 1, 1, along, 'wrap'), along)

def block_forward(source, inverses, lower_maps, upper_maps):
    size_block = inverses.shape[-1]
    block_total = inverses.shape[1]

    def apply_matrix(matrix, vector):
        return jnp.einsum('aij,jab->iab', matrix, vector, precision=lax.Precision.HIGHEST)
    solved = []
    for index in range(block_total):
        block_rhs = source[index * size_block:(index + 1) * size_block]
        if index > 0:
            block_rhs = block_rhs - apply_matrix(lower_maps[:, index - 1], solved[-1])
        solved.append(apply_matrix(inverses[:, index], block_rhs))
    result_blocks = [solved[-1]]
    for index in range(block_total - 2, -1, -1):
        result_blocks.insert(0, solved[index] - apply_matrix(upper_maps[:, index], result_blocks[0]))
    return jnp.concatenate(result_blocks, 0)

def transpose_of(forward, cotangent):
    return jax.vjp(forward, jnp.zeros_like(cotangent))[1](cotangent)[0]

def slot_rows(owner, capacity):
    count = owner.shape[0]
    same_owner = owner[:, None] == owner[None, :]
    earlier = jnp.arange(count)[None, :] < jnp.arange(count)[:, None]
    slot_rank = lax.optimization_barrier(jnp.sum((same_owner & earlier).astype(jnp.int32), axis=1))
    return (owner * capacity + slot_rank).astype(jnp.int32)

def reference(adjoint_in, courant_lon, codes_lon, courant_lat, codes_lat, courant_lev, codes_lev, block_inverse, block_lower, block_upper, region_ids, owner):
    adjoint = adjoint_in
    for substep in range(SUB):
        adjoint = transpose_of(lambda tracer: wall_forward(tracer, courant_lat, codes_lat, 1), adjoint)
        adjoint = transpose_of(lambda tracer: cycle_forward(tracer, courant_lon, codes_lon, 2), adjoint)
    adjoint = transpose_of(lambda tracer: block_forward(tracer, block_inverse, block_lower, block_upper), adjoint)
    adjoint = transpose_of(lambda tracer: wall_forward(tracer, courant_lev, codes_lev, 0), adjoint)
    columns = adjoint.reshape(NLEV, NLAT * NLON).T
    weight_scale = (NREG / (NLAT * NLON)) ** 0.5
    region_sums = jax.ops.segment_sum(columns, region_ids.reshape(-1), num_segments=NREG) * weight_scale
    row_index = slot_rows(owner, REG_MOST)
    region_sens = jnp.zeros((N_LAT * N_LEV * REG_MOST, NLEV), jnp.float32).at[row_index].set(region_sums)
    return (adjoint, region_sens)
```

```python
import functools

import jax
import jax.numpy as jnp
from jax import lax
from jax.experimental import pallas as pl
from jax.experimental.pallas import tpu as pltpu
from jax.sharding import PartitionSpec as P

SUB = 2
SLOTS = 16
LANES = 128
F32 = jnp.float32
BF16 = jnp.bfloat16
VMEM = pl.BlockSpec(memory_space=pltpu.VMEM)
SMEM = pl.BlockSpec(memory_space=pltpu.SMEM)
NT = (((1,), (1,)), ((), ()))


def params():
    return pltpu.CompilerParams(vmem_limit_bytes=40 * 2**20)


def flux_parts(courant):
    up = jnp.maximum(courant, 0.0)
    down = jnp.minimum(courant, 0.0)
    half = 0.5 * courant
    return up, down, up * (0.5 - half), down * (0.5 + half)


def slope_parts(codes):
    centred = jnp.where(codes == 3, 0.5, 0.0)
    ahead = jnp.where(codes == 1, 1.0, centred)
    behind = jnp.where(codes == 2, 1.0, centred)
    return ahead, behind


def split(value):
    high = value.astype(BF16)
    low = (value - high.astype(F32)).astype(BF16)
    return high, low


def roll(value, shift, axis):
    return pltpu.roll(value, shift % value.shape[axis], axis)


def wrapped(value, width):
    length = value.shape[1]
    spare = width - length
    first = spare // 2
    return jnp.concatenate([value, value[:, :first], value[:, length - spare + first :]], axis=1)


def horizontal_kernel(
    last_ref, a_ref, clat_ref, klat_ref, clon_ref, klon_ref, below_ref, above_ref, bcoef_ref, acoef_ref, *refs, final
):
    if final:
        send_ref, edge_w, edge_q, edge_a, edge_r, rows_ref = refs
    else:
        out_ref, up_ref, down_ref, edge_w, edge_q, edge_a, edge_r, rows_ref = refs
    levels, rows, lons = a_ref.shape
    width = rows_ref.shape[2]
    last = last_ref[0]
    a0 = a_ref[:, 0, :]
    am1, am2 = below_ref[0], below_ref[1]
    up1, down1, uph1, downh1 = flux_parts(bcoef_ref[0])
    _, _, _, downh2 = flux_parts(bcoef_ref[1])
    ahead1, _ = slope_parts(bcoef_ref[2])
    f1 = a0 - am1
    f2 = am1 - am2
    s1 = uph1 * f1 - downh2 * f2
    edge_w[...] = downh1 * f1
    edge_q[...] = down1 * f1 + ahead1 * s1
    a_in = a_ref[:, rows - 1, :]
    a16, a17 = above_ref[0], above_ref[1]
    c15 = jnp.where(last == 1, 0.0, clat_ref[:, rows - 1, :])
    _, _, _, downh15 = flux_parts(c15)
    _, _, uph16, _ = flux_parts(acoef_ref[0])
    _, behind16 = slope_parts(acoef_ref[1])
    edge_a[...] = a16
    edge_r[...] = behind16 * (uph16 * (a17 - a16) - downh15 * (a16 - a_in))

    step = 4 * LANES
    chunks = [(start, min(step, lons - start)) for start in range(0, lons, step)]
    tile = 8

    def level(l, carry):
        for start, size in chunks:
            cols = slice(start, start + size)
            row = lax.broadcasted_iota(jnp.int32, (rows, size), 0)
            lowest, highest = row == 0, row == rows - 1
            a = a_ref[l, :, cols]
            courant = jnp.where(highest & (last == 1), 0.0, clat_ref[l, :, cols])
            up, down, uph, downh = flux_parts(courant)
            ahead, behind = slope_parts(klat_ref[l, :, cols])

            def edge(ref):
                return ref[pl.ds(l, 1), cols]

            f = jnp.where(highest, edge(edge_a), roll(a, -1, 0)) - a
            s = uph * f - jnp.where(lowest, edge(edge_w), roll(downh * f, 1, 0))
            q = jnp.where(lowest, edge(edge_q), roll(down * f + ahead * s, 1, 0))
            r = jnp.where(highest, edge(edge_r), roll(behind * s, -1, 0))
            rows_ref[0, :, cols] = a + up * f + (behind - ahead) * s + q - r
        for low in range(0, rows, tile):
            band = slice(low, low + tile)
            a = wrapped(rows_ref[0, band, :lons], width)
            up, down, uph, downh = flux_parts(wrapped(clon_ref[l, band, :], width))
            ahead, behind = slope_parts(wrapped(klon_ref[l, band, :], width))
            f = roll(a, -1, 1) - a
            s = uph * f - roll(downh * f, 1, 1)
            q = roll(down * f + ahead * s, 1, 1)
            r = roll(behind * s, -1, 1)
            value = a + up * f + (behind - ahead) * s + q - r
            if final:
                parts = send_ref.shape[0]
                share = lons // parts
                for part in range(parts):
                    send_ref[part, l, band, :] = value[:, part * share : (part + 1) * share]
            else:
                out_ref[l, band, :] = value[:, :lons]
        return carry

    lax.fori_loop(0, levels, level, 0)
    if not final:
        up_ref[0] = out_ref[:, rows - 1, :]
        up_ref[1] = out_ref[:, rows - 2, :]
        down_ref[0] = out_ref[:, 0, :]
        down_ref[1] = out_ref[:, 1, :]


def horizontal(last, a, clat, klat, clon, klon, below, above, bcoef, acoef, parts):
    levels, rows, lons = a.shape
    width = -(-lons // LANES) * LANES
    final = parts > 0
    if final:
        out_shape = jax.ShapeDtypeStruct((parts, levels, rows, lons // parts), F32)
    else:
        edge = jax.ShapeDtypeStruct((2, levels, lons), F32)
        out_shape = (jax.ShapeDtypeStruct(a.shape, F32), edge, edge)
    return pl.pallas_call(
        functools.partial(horizontal_kernel, final=final),
        out_shape=out_shape,
        in_specs=[SMEM] + [VMEM] * 9,
        out_specs=VMEM if final else (VMEM, VMEM, VMEM),
        scratch_shapes=[pltpu.VMEM((levels, lons), F32)] * 4 + [pltpu.VMEM((1, rows, width), F32)],
        compiler_params=params(),
        name="horizontal",
    )(last, a, clat, klat, clon, klon, below, above, bcoef, acoef)


def prep_kernel(inverse_ref, lower_ref, upper_ref, owner_ref, matrix_ref, slot_ref, *, devices):
    lats, blocks, size, _ = inverse_ref.shape
    group = LANES // size
    levels = blocks * size
    row = lax.broadcasted_iota(jnp.int32, (LANES, LANES), 0)
    col = lax.broadcasted_iota(jnp.int32, (LANES, LANES), 1)
    diagonal = (row // size) == (col // size)
    row_l = lax.broadcasted_iota(jnp.int32, (LANES, levels), 0)
    col_l = lax.broadcasted_iota(jnp.int32, (LANES, levels), 1)

    def times(matrix, vector):
        wide = jnp.concatenate([matrix.reshape(LANES, size)] * group, axis=1)
        wide = jnp.where(diagonal, wide, 0.0)
        return jnp.dot(wide, vector, precision=lax.Precision.HIGHEST, preferred_element_type=F32)

    for first in range(0, lats, group):
        lat = slice(first, first + group)
        solved = []
        for k in range(blocks):
            rhs = jnp.where(col_l == row_l % size + size * k, 1.0, 0.0)
            if k > 0:
                rhs = rhs - times(lower_ref[lat, k - 1], solved[-1])
            solved.append(times(inverse_ref[lat, k], rhs))
        result = [solved[-1]]
        for k in range(blocks - 2, -1, -1):
            result.insert(0, solved[k] - times(upper_ref[lat, k], result[0]))
        for g in range(group):
            dense = jnp.concatenate([block[g * size : (g + 1) * size] for block in result], axis=0)
            high, low = split(dense.T)
            matrix_ref[first + g] = jnp.concatenate([high, low, high], axis=1)

    tiles = owner_ref.shape[0]
    device = lax.broadcasted_iota(jnp.int32, (devices, LANES), 0)
    earlier = jnp.where(row < col, 1.0, 0.0).astype(BF16)
    running = jnp.zeros((devices, 1), F32)
    for t in range(tiles):
        owned = jnp.where(owner_ref[pl.ds(t, 1), :] == device, 1.0, 0.0)
        before = jnp.dot(owned.astype(BF16), earlier, preferred_element_type=F32) + running
        slot_ref[pl.ds(t, 1), :] = jnp.sum(owned * before, axis=0, keepdims=True).astype(jnp.int32)
        running = running + jnp.sum(owned, axis=1, keepdims=True)


def prep(inverse, lower, upper, owner_tiles, devices):
    lats, blocks, size, _ = inverse.shape
    levels = blocks * size
    return pl.pallas_call(
        functools.partial(prep_kernel, devices=devices),
        out_shape=(
            jax.ShapeDtypeStruct((lats, levels, 3 * levels), BF16),
            jax.ShapeDtypeStruct(owner_tiles.shape, jnp.int32),
        ),
        in_specs=[VMEM] * 4,
        out_specs=(VMEM, VMEM),
        compiler_params=params(),
        name="prep",
    )(inverse, lower, upper, owner_tiles)


def vertical_kernel(x_ref, matrix_ref, c_ref, k_ref, out_ref, y_ref):
    levels, rows, _ = x_ref.shape
    for lat in range(rows):
        high, low = split(x_ref[:, lat, :])
        stacked = jnp.concatenate([high, high, low], axis=0)
        y_ref[:, lat, :] = jnp.dot(matrix_ref[lat], stacked, preferred_element_type=F32)
    zero = jnp.zeros(x_ref.shape[1:], F32)
    y = y_ref[0]
    prior_w, prior_q, pending = zero, zero, None
    for i in range(levels):
        ahead, behind = slope_parts(k_ref[i])
        if i < levels - 1:
            up, down, uph, downh = flux_parts(c_ref[i])
            y_next = y_ref[i + 1]
            f = y_next - y
            s = uph * f - prior_w
            here = y + up * f + prior_q
            prior_w = downh * f
            prior_q = down * f + ahead * s
        else:
            y_next = None
            s = -prior_w
            here = y + prior_q
        here = here + (behind - ahead) * s
        if i > 0:
            out_ref[i - 1] = pending - behind * s
        pending = here
        y = y_next
    out_ref[levels - 1] = pending


def vertical(x, matrix, courant, codes):
    return pl.pallas_call(
        vertical_kernel,
        out_shape=jax.ShapeDtypeStruct(x.shape, F32),
        in_specs=[VMEM] * 4,
        out_specs=VMEM,
        scratch_shapes=[pltpu.VMEM(x.shape, F32)],
        compiler_params=params(),
        name="vertical",
    )(x, matrix, courant, codes)


def region_kernel(field_ref, ids_ref, owner_ref, slot_ref, out_ref, send_ref, high_ref, low_ref, acc_ref, table_ref, *, scale):
    parts, levels, rows, share = field_ref.shape
    tiles = owner_ref.shape[0]
    devices = send_ref.shape[0]
    lons = parts * share
    for l in range(levels):
        whole = jnp.concatenate([field_ref[part, l] for part in range(parts)], axis=1)
        out_ref[l] = whole
        high = whole.astype(BF16).astype(F32)
        high_ref[l] = high
        low_ref[l] = whole - high
    acc_ref[...] = jnp.zeros_like(acc_ref)
    coarse = lax.broadcasted_iota(jnp.int32, (tiles, lons), 0)
    fine = lax.broadcasted_iota(jnp.int32, (LANES, lons), 0)

    def band(lat, carry):
        ids = ids_ref[pl.ds(lat, 1), :]
        mask = (ids // LANES) == coarse
        onehot = jnp.where((ids % LANES) == fine, 1.0, 0.0).astype(BF16)
        pieces = []
        for ref in (high_ref, low_ref):
            for l in range(levels):
                pieces.append(jnp.where(mask, ref[l, pl.ds(lat, 1), :], 0.0).astype(BF16))
        stacked = jnp.concatenate(pieces, axis=0)
        acc_ref[...] += lax.dot_general(stacked, onehot, NT, preferred_element_type=F32)
        return carry

    lax.fori_loop(0, rows, band, 0)
    half = levels * tiles
    table_ref[...] = acc_ref[pl.ds(0, half), :] + acc_ref[pl.ds(half, half), :]
    device = lax.broadcasted_iota(jnp.int32, (devices, LANES), 0)
    place = lax.broadcasted_iota(jnp.int32, (SLOTS * levels, LANES), 0) // levels
    total = jnp.zeros((devices, SLOTS * levels), F32)
    for t in range(tiles):
        owned = jnp.where(owner_ref[pl.ds(t, 1), :] == device, 1.0, 0.0).astype(BF16)
        sums = table_ref[pl.ds(t, levels, stride=tiles), :]
        spread = jnp.where(slot_ref[pl.ds(t, 1), :] == place, jnp.concatenate([sums] * SLOTS, axis=0), 0.0)
        for piece in split(spread):
            total += lax.dot_general(owned, piece, NT, preferred_element_type=F32)
    send_ref[...] = total * scale


def regions(field, ids, owner_tiles, slot_tiles, devices, scale):
    parts, levels, rows, share = field.shape
    tiles = owner_tiles.shape[0]
    lons = parts * share
    return pl.pallas_call(
        functools.partial(region_kernel, scale=scale),
        out_shape=(
            jax.ShapeDtypeStruct((levels, rows, lons), F32),
            jax.ShapeDtypeStruct((devices, SLOTS * levels), F32),
        ),
        in_specs=[VMEM] * 4,
        out_specs=(VMEM, VMEM),
        scratch_shapes=[
            pltpu.VMEM((levels, rows, lons), F32),
            pltpu.VMEM((levels, rows, lons), F32),
            pltpu.VMEM((2 * levels * tiles, LANES), F32),
            pltpu.VMEM((levels * tiles, LANES), F32),
        ],
        compiler_params=params(),
        name="regions",
    )(field, ids, owner_tiles, slot_tiles)


def neighbours(up, down):
    count = lax.axis_size("lat")
    forward = [(i, i + 1) for i in range(count - 1)]
    backward = [(target, source) for source, target in forward]
    return lax.ppermute(up, "lat", forward), lax.ppermute(down, "lat", backward)


def local(
    adjoint_in,
    courant_lon,
    codes_lon,
    courant_lat,
    codes_lat,
    courant_lev,
    codes_lev,
    block_inverse,
    block_lower,
    block_upper,
    region_ids,
    owner,
):
    levels_here, bands_here, lon_cells = adjoint_in.shape
    band_count = lax.axis_size("lat")
    group_count = lax.axis_size("lev")
    devices = band_count * group_count
    region_count = owner.shape[0]
    tiles = -(-region_count // LANES)
    tiles = -(-tiles // 8) * 8
    owner_tiles = jnp.pad(owner, (0, tiles * LANES - region_count), constant_values=-1).reshape(tiles, LANES)
    matrix, slot_tiles = prep(block_inverse, block_lower, block_upper, owner_tiles, devices)
    last = (lax.axis_index("lat") == band_count - 1).astype(jnp.int32).reshape(1)
    edge = bands_here - 1
    up = jnp.stack(
        [
            adjoint_in[:, edge],
            adjoint_in[:, edge - 1],
            courant_lat[:, edge],
            courant_lat[:, edge - 1],
            codes_lat[:, edge].astype(F32),
        ]
    )
    down = jnp.stack([adjoint_in[:, 0], adjoint_in[:, 1], courant_lat[:, 0], codes_lat[:, 0].astype(F32)])
    below, above = neighbours(up, down)
    coefficients = (courant_lat, codes_lat, courant_lon, codes_lon)
    adjoint, up, down = horizontal(
        last, adjoint_in, *coefficients, below[:2], above[:2], below[2:], above[2:], 0
    )
    below_next, above_next = neighbours(up, down)
    sent = horizontal(
        last, adjoint, *coefficients, below_next, above_next, below[2:], above[2:], group_count
    )
    columns = lax.all_to_all(sent, "lev", split_axis=0, concat_axis=0, tiled=True)
    columns = columns.reshape(group_count * levels_here, bands_here, lon_cells // group_count)
    columns = vertical(columns, matrix, courant_lev, codes_lev)
    columns = columns.reshape(group_count, levels_here, bands_here, lon_cells // group_count)
    field = lax.all_to_all(columns, "lev", split_axis=0, concat_axis=0, tiled=True)
    scale = (region_count / (bands_here * band_count * lon_cells)) ** 0.5
    adjoint_out, rows = regions(field, region_ids, owner_tiles, slot_tiles, devices, scale)
    rows = lax.all_to_all(rows, ("lat", "lev"), split_axis=0, concat_axis=0, tiled=True)
    rows = jnp.sum(rows.reshape(band_count, group_count, SLOTS, levels_here), axis=0)
    region_sens = jnp.transpose(rows, (1, 0, 2)).reshape(SLOTS, group_count * levels_here)
    return (adjoint_out, region_sens)


def solution(mesh):
    placed = (
        P("lev", "lat", None),
        P("lev", "lat", None),
        P("lev", "lat", None),
        P("lev", "lat", None),
        P("lev", "lat", None),
        P(None, "lat", "lev"),
        P(None, "lat", "lev"),
        P("lat", None, None, None),
        P("lat", None, None, None),
        P("lat", None, None, None),
        P("lat", None),
        P(),
    )
    return jax.shard_map(
        local,
        mesh=mesh,
        in_specs=placed,
        out_specs=(P("lev", "lat", None), P(("lat", "lev"), None)),
        check_vma=False,
    )
```

```python
import functools

import jax
import jax.numpy as jnp
from jax import lax
from jax.experimental import pallas as pl
from jax.experimental.pallas import tpu as pltpu
from jax.sharding import PartitionSpec as P

SUB = 2
SLOTS = 16
LANES = 128
HALF = LANES // 2
F32 = jnp.float32
BF16 = jnp.bfloat16
VMEM = pl.BlockSpec(memory_space=pltpu.VMEM)
SMEM = pl.BlockSpec(memory_space=pltpu.SMEM)
HBM = pl.BlockSpec(memory_space=pltpu.HBM)


def params(mib=20):
    return pltpu.CompilerParams(vmem_limit_bytes=mib * 2**20)


def cost(microseconds):
    return pl.CostEstimate(flops=microseconds * 10**9, bytes_accessed=microseconds * 10**6, transcendentals=0)


def flux_parts(courant):
    up = jnp.maximum(courant, 0.0)
    down = jnp.minimum(courant, 0.0)
    half = 0.5 * courant
    return up, down, up * (0.5 - half), down * (0.5 + half)


def slope_parts(codes):
    centred = jnp.where(codes == 3, 0.5, 0.0)
    ahead = jnp.where(codes == 1, 1.0, centred)
    behind = jnp.where(codes == 2, 1.0, centred)
    return ahead, behind


def split(value):
    high = value.astype(BF16)
    low = (value - high.astype(F32)).astype(BF16)
    return high, low


def roll(value, shift, axis):
    return pltpu.roll(value, shift % value.shape[axis], axis)


def wrapped(value, width):
    length = value.shape[1]
    spare = width - length
    first = spare // 2
    return jnp.concatenate([value, value[:, :first], value[:, length - spare + first :]], axis=1)


def sweep_lon(value, up, down, uph, downh, ahead, behind):
    f = roll(value, -1, 1) - value
    s = uph * f - roll(downh * f, 1, 1)
    q = roll(down * f + ahead * s, 1, 1)
    r = roll(behind * s, -1, 1)
    return value + up * f + (behind - ahead) * s + q - r


def lon_parts(courant, codes, width):
    return (*flux_parts(wrapped(courant, width)), *slope_parts(wrapped(codes, width)))


def edge_rows(rows):
    return (0, 1, rows - 2, rows - 1)


def interior_kernel(last_ref, *refs, final):
    if final:
        a_ref, up_ref, down_ref, clat_ref, klat_ref, clon_ref, klon_ref, send_ref, swept_ref, rows_ref = refs
    else:
        a_ref, clat_ref, klat_ref, clon_ref, klon_ref, out_ref, swept_ref, edge_ref, lonc_ref, rows_ref = refs
    levels, rows, lons = a_ref.shape
    width = rows_ref.shape[2]
    half = levels // 2
    last = last_ref[0]
    step = 4 * LANES
    chunks = [(start, min(step, lons - start)) for start in range(0, lons, step)]
    tile = 8

    def level(l, upper):
        for start, size in chunks:
            cols = slice(start, start + size)
            row = lax.broadcasted_iota(jnp.int32, (rows, size), 0)
            lowest, highest = row == 0, row == rows - 1
            a = a_ref[l, :, cols]
            if final:
                a = jnp.where(lowest, down_ref[0, pl.ds(l, 1), cols], a)
                a = jnp.where(row == 1, down_ref[1, pl.ds(l, 1), cols], a)
                a = jnp.where(row == rows - 2, up_ref[1, pl.ds(l, 1), cols], a)
                a = jnp.where(highest, up_ref[0, pl.ds(l, 1), cols], a)
            courant = jnp.where(highest & (last == 1), 0.0, clat_ref[l, :, cols])
            up, down, uph, downh = flux_parts(courant)
            ahead, behind = slope_parts(klat_ref[l, :, cols])
            f = jnp.where(highest, 0.0, roll(a, -1, 0)) - a
            s = uph * f - jnp.where(lowest, 0.0, roll(downh * f, 1, 0))
            q = jnp.where(lowest, 0.0, roll(down * f + ahead * s, 1, 0))
            r = jnp.where(highest, 0.0, roll(behind * s, -1, 0))
            rows_ref[l, :, cols] = a + up * f + (behind - ahead) * s + q - r
        for low in range(0, rows, tile):
            band = slice(low, low + tile)
            value = sweep_lon(
                wrapped(rows_ref[l, band, :lons], width), *lon_parts(clon_ref[l, band, :], klon_ref[l, band, :], width)
            )
            if final:
                parts = send_ref.shape[0]
                share = lons // parts
                for part in range(parts):
                    start = part * share
                    send_ref[part, l, band, :] = value[:, start : start + LANES]
                    rest = value[:, start + LANES : start + share]
                    if upper:
                        send_ref[part, half + l, band, HALF : HALF + share - LANES] = rest
                    else:
                        send_ref[part, levels + l, band, : share - LANES] = rest
            else:
                out_ref[l, band, :] = value[:, :lons]

    def pair(index, carry):
        level(index, False)
        level(index + half, True)
        return carry

    lax.fori_loop(0, half, pair, 0)
    for n, row in enumerate(edge_rows(rows)):
        swept_ref[n] = rows_ref[:, row, :lons]
    if not final:
        high = rows - 1
        courant = jnp.where(last == 1, 0.0, clat_ref[:, high, :])
        up, _, uph, downh = flux_parts(courant)
        ahead, behind = slope_parts(klat_ref[:, high, :])
        ahead0, behind0 = slope_parts(klat_ref[:, 0, :])
        edge_ref[0] = a_ref[:, 0, :]
        edge_ref[1] = a_ref[:, high, :]
        edge_ref[2] = behind0 - ahead0
        edge_ref[3] = ahead0
        edge_ref[4] = up + (behind - ahead) * uph
        edge_ref[5] = behind * uph
        edge_ref[6] = downh
        for n, row in enumerate(edge_rows(rows)):
            for m, part in enumerate(lon_parts(clon_ref[:, row, :], klon_ref[:, row, :], width)):
                lonc_ref[n, m] = part


def interior(last, fields, coefficients, parts):
    levels, rows, lons = fields[0].shape
    width = -(-lons // LANES) * LANES
    final = parts > 0
    whole = (levels, rows, lons)
    swept = jax.ShapeDtypeStruct((4, levels, lons), F32)
    if final:
        out_shape = (jax.ShapeDtypeStruct((parts, levels + levels // 2, rows, LANES), F32), swept)
    else:
        out_shape = (
            jax.ShapeDtypeStruct(whole, F32),
            swept,
            jax.ShapeDtypeStruct((7, levels, lons), F32),
            jax.ShapeDtypeStruct((4, 6, levels, width), F32),
        )
    return pl.pallas_call(
        functools.partial(interior_kernel, final=final),
        out_shape=out_shape,
        in_specs=[SMEM] + [VMEM] * (len(fields) + len(coefficients)),
        out_specs=(VMEM,) * len(out_shape),
        scratch_shapes=[pltpu.VMEM((levels, rows, width), F32)],
        compiler_params=params(),
        cost_estimate=cost(4),
        name="interior",
    )(last, *fields, *coefficients)


def edges_kernel(below_ref, above_ref, edge_ref, lonc_ref, swept_ref, *refs, final):
    width = lonc_ref.shape[3]
    _, levels, lons = swept_ref.shape
    if final:
        below_next, above_next, up_in, down_in, sent_ref, send_ref, main_ref, rest_ref = refs
        row0, row15 = down_in[0], up_in[0]
        am1, am2, a16, a17 = below_next[0], below_next[1], above_next[0], above_next[1]
    else:
        up_ref, down_ref = refs
        row0, row15 = edge_ref[0], edge_ref[1]
        am1, am2, a16, a17 = below_ref[0], below_ref[1], above_ref[0], above_ref[1]
    _, down1, uph1, downh1 = flux_parts(below_ref[2])
    _, _, _, downh2 = flux_parts(below_ref[3])
    ahead1, _ = slope_parts(below_ref[4])
    f1 = row0 - am1
    w = downh1 * f1
    q = down1 * f1 + ahead1 * (uph1 * f1 - downh2 * (am1 - am2))
    _, _, uph16, _ = flux_parts(above_ref[2])
    _, behind16 = slope_parts(above_ref[3])
    r = behind16 * (uph16 * (a17 - a16) - edge_ref[6] * (a16 - row15))
    fixed = (
        swept_ref[0] - edge_ref[2] * w + q,
        swept_ref[1] - edge_ref[3] * w,
        swept_ref[2] - edge_ref[5] * a16,
        swept_ref[3] + edge_ref[4] * a16 - r,
    )
    rows = []
    for n, row in enumerate(fixed):
        rows.append(sweep_lon(wrapped(row, width), *(lonc_ref[n, m] for m in range(6))))
    if final:
        parts, _, count, _ = send_ref.shape
        share = lons // parts
        half = levels // 2
        tile = 8
        sublane = lax.broadcasted_iota(jnp.int32, (tile, LANES), 0)
        lower = lax.broadcasted_iota(jnp.int32, (tile, LANES), 1) < HALF
        first = lax.broadcasted_iota(jnp.int32, (levels, LANES), 0) < half
        blank = jnp.zeros((levels, LANES - (share - LANES)), F32)

        for n, row in enumerate(rows):
            for part in range(parts):
                start = part * share
                main_ref[n, part] = row[:, start : start + LANES]
                rest = jnp.concatenate([row[:, start + LANES : start + share], blank], axis=1)
                rest_ref[n, part] = jnp.where(first, rest, roll(rest, HALF, 1))
        places = edge_rows(count)
        for low in range(0, count, tile):
            band = slice(low, low + tile)
            mine = [(n, place - low) for n, place in enumerate(places) if low <= place < low + tile]
            for part in range(parts):
                for l in range(levels):
                    value = sent_ref[part, l, band, :]
                    for n, place in mine:
                        value = jnp.where(sublane == place, main_ref[n, part, l : l + 1, :], value)
                    send_ref[part, l, band, :] = value
                for l in range(half):
                    value = sent_ref[part, levels + l, band, :]
                    for n, place in mine:
                        both = jnp.where(
                            lower, rest_ref[n, part, l : l + 1, :], rest_ref[n, part, l + half : l + half + 1, :]
                        )
                        value = jnp.where(sublane == place, both, value)
                    send_ref[part, levels + l, band, :] = value
    else:
        down_ref[0], down_ref[1] = rows[0][:, :lons], rows[1][:, :lons]
        up_ref[0], up_ref[1] = rows[3][:, :lons], rows[2][:, :lons]


def edges(below, above, edge, lonc, swept, *more):
    _, levels, lons = swept.shape
    final = len(more) > 0
    args = (below, above, edge, lonc, swept, *more)
    if final:
        out_shape = jax.ShapeDtypeStruct(more[-1].shape, F32)
        scratch = [pltpu.VMEM((4, more[-1].shape[0], levels, LANES), F32)] * 2
    else:
        out_shape = (jax.ShapeDtypeStruct((2, levels, lons), F32),) * 2
        scratch = []
    return pl.pallas_call(
        functools.partial(edges_kernel, final=final),
        out_shape=out_shape,
        in_specs=[VMEM] * len(args),
        out_specs=VMEM if final else (VMEM, VMEM),
        scratch_shapes=scratch,
        compiler_params=params(),
        cost_estimate=cost(1),
        name="edges",
    )(*args)


def pack_kernel(*refs):
    *sources, up_ref, down_ref, a_ref, clat_ref, klat_ref, sems = refs
    fields = (a_ref, clat_ref, klat_ref)
    levels, rows, _ = a_ref.shape
    half = levels // 2
    copies = []
    for n, (src, dst) in enumerate(zip(sources, fields)):
        for part in range(2):
            span = pl.ds(part * half, half)
            copies.append(pltpu.make_async_copy(src.at[span], dst.at[span], sems.at[n, part]))
    for copy in copies:
        copy.start()
    for copy in copies:
        copy.wait()
    edge = rows - 1
    up_ref[0] = a_ref[:, edge, :]
    up_ref[1] = a_ref[:, edge - 1, :]
    down_ref[0] = a_ref[:, 0, :]
    down_ref[1] = a_ref[:, 1, :]
    up_ref[2] = clat_ref[:, edge, :]
    up_ref[3] = clat_ref[:, edge - 1, :]
    down_ref[2] = clat_ref[:, 0, :]
    up_ref[4] = klat_ref[:, edge, :].astype(F32)
    down_ref[3] = klat_ref[:, 0, :].astype(F32)


def pack(a, clat, klat):
    levels, _, lons = a.shape
    return pl.pallas_call(
        pack_kernel,
        out_shape=(jax.ShapeDtypeStruct((5, levels, lons), F32), jax.ShapeDtypeStruct((4, levels, lons), F32)),
        in_specs=[HBM] * 3,
        out_specs=(VMEM, VMEM),
        scratch_shapes=[pltpu.VMEM(a.shape, x.dtype) for x in (a, clat, klat)] + [pltpu.SemaphoreType.DMA((3, 2))],
        compiler_params=params(60),
        cost_estimate=cost(2),
        name="pack",
    )(a, clat, klat)


def prep_kernel(
    inverse_ref, lower_ref, upper_ref, owner_ref, ids_ref, matrix_ref, slot_ref, fine_ref, device_ref, *, devices
):
    lats, blocks, size, _ = inverse_ref.shape
    group = LANES // size
    levels = blocks * size
    row = lax.broadcasted_iota(jnp.int32, (LANES, LANES), 0)
    col = lax.broadcasted_iota(jnp.int32, (LANES, LANES), 1)
    diagonal = (row // size) == (col // size)
    row_l = lax.broadcasted_iota(jnp.int32, (LANES, levels), 0)
    col_l = lax.broadcasted_iota(jnp.int32, (LANES, levels), 1)

    def times(matrix, vector):
        wide = jnp.concatenate([matrix.reshape(LANES, size)] * group, axis=1)
        wide = jnp.where(diagonal, wide, 0.0)
        return jnp.dot(wide, vector, precision=lax.Precision.HIGHEST, preferred_element_type=F32)

    for first in range(0, lats, group):
        lat = slice(first, first + group)
        solved = []
        for k in range(blocks):
            rhs = jnp.where(col_l == row_l % size + size * k, 1.0, 0.0)
            if k > 0:
                rhs = rhs - times(lower_ref[lat, k - 1], solved[-1])
            solved.append(times(inverse_ref[lat, k], rhs))
        result = [solved[-1]]
        for k in range(blocks - 2, -1, -1):
            result.insert(0, solved[k] - times(upper_ref[lat, k], result[0]))
        for g in range(group):
            dense = jnp.concatenate([block[g * size : (g + 1) * size] for block in result], axis=0)
            high, low = split(dense.T)
            matrix_ref[first + g] = jnp.concatenate([high, low, high], axis=1)

    tiles = owner_ref.shape[0]
    device = lax.broadcasted_iota(jnp.int32, (devices, LANES), 0)
    earlier = jnp.where(row < col, 1.0, 0.0).astype(BF16)
    running = jnp.zeros((devices, 1), F32)
    for t in range(tiles):
        owned = jnp.where(owner_ref[pl.ds(t, 1), :] == device, 1.0, 0.0)
        before = jnp.dot(owned.astype(BF16), earlier, preferred_element_type=F32) + running
        slot_ref[pl.ds(t, 1), :] = jnp.sum(owned * before, axis=0, keepdims=True).astype(jnp.int32)
        running = running + jnp.sum(owned, axis=1, keepdims=True)
    fine_ref[...] = (ids_ref[...] % LANES).astype(F32).T
    device_ref[...] = owner_ref[...].astype(F32).T


def prep(inverse, lower, upper, owner_tiles, ids, devices):
    lats, blocks, size, _ = inverse.shape
    levels = blocks * size
    return pl.pallas_call(
        functools.partial(prep_kernel, devices=devices),
        out_shape=(
            jax.ShapeDtypeStruct((lats, levels, 3 * levels), BF16),
            jax.ShapeDtypeStruct(owner_tiles.shape, jnp.int32),
            jax.ShapeDtypeStruct(ids.shape[::-1], F32),
            jax.ShapeDtypeStruct(owner_tiles.shape[::-1], F32),
        ),
        in_specs=[VMEM] * 5,
        out_specs=(VMEM,) * 4,
        compiler_params=params(),
        cost_estimate=cost(5),
        name="prep",
    )(inverse, lower, upper, owner_tiles, ids)


def unpacked(main, rest, upper, spare):
    if upper:
        rest = roll(rest, HALF, rest.ndim - 1)
    return jnp.concatenate([main, rest[..., :spare]], axis=-1)


def vertical_kernel(x_ref, matrix_ref, c_ref, k_ref, out_ref, field_ref, y_ref):
    levels, rows, share = c_ref.shape
    parts = x_ref.shape[0]
    group = levels // parts
    half = group // 2
    spare = share - LANES
    for level in range(levels):
        part, l = level // group, level % group
        field_ref[level] = unpacked(x_ref[part, l], x_ref[part, group + l % half], l // half, spare)
    for lat in range(rows):
        high, low = split(field_ref[:, lat, :])
        stacked = jnp.concatenate([high, high, low], axis=0)
        y_ref[:, lat, :] = jnp.dot(matrix_ref[lat], stacked, preferred_element_type=F32)

    def emit(level, value):
        part, l = level // group, level % group
        out_ref[part, l] = value[:, :LANES]
        place = group + l % half
        if l // half:
            out_ref[part, place, :, HALF : HALF + spare] = value[:, LANES:]
        else:
            out_ref[part, place, :, :spare] = value[:, LANES:]

    zero = jnp.zeros((rows, share), F32)
    y = y_ref[0]
    prior_w, prior_q, pending = zero, zero, None
    for i in range(levels):
        ahead, behind = slope_parts(k_ref[i])
        if i < levels - 1:
            up, down, uph, downh = flux_parts(c_ref[i])
            y_next = y_ref[i + 1]
            f = y_next - y
            s = uph * f - prior_w
            here = y + up * f + prior_q
            prior_w = downh * f
            prior_q = down * f + ahead * s
        else:
            y_next = None
            s = -prior_w
            here = y + prior_q
        here = here + (behind - ahead) * s
        if i > 0:
            emit(i - 1, pending - behind * s)
        pending = here
        y = y_next
    emit(levels - 1, pending)


def vertical(x, matrix, courant, codes):
    return pl.pallas_call(
        vertical_kernel,
        out_shape=jax.ShapeDtypeStruct(x.shape, F32),
        in_specs=[VMEM] * 4,
        out_specs=VMEM,
        scratch_shapes=[pltpu.VMEM(courant.shape, F32)] * 2,
        compiler_params=params(),
        cost_estimate=cost(5),
        name="vertical",
    )(x, matrix, courant, codes)


def region_kernel(
    field_ref, ids_ref, fine_ref, device_ref, slot_ref, out_ref, send_ref, high_ref, low_ref, acc_ref, table_ref, *, scale
):
    levels, rows, lons = out_ref.shape
    parts = field_ref.shape[0]
    share = lons // parts
    half = levels // 2
    tiles = slot_ref.shape[0]
    devices = send_ref.shape[0]
    for l in range(levels):
        pieces = [
            unpacked(field_ref[part, l], field_ref[part, levels + l % half], l // half, share - LANES)
            for part in range(parts)
        ]
        whole = jnp.concatenate(pieces, axis=1)
        out_ref[l] = whole
        high = whole.astype(BF16).astype(F32)
        high_ref[l] = high
        low_ref[l] = whole - high
    coarse = lax.broadcasted_iota(jnp.int32, (tiles, lons), 0)
    lane = lax.broadcasted_iota(jnp.int32, (lons, LANES), 1).astype(F32)
    for lat in range(rows):
        mask = jnp.where((ids_ref[lat : lat + 1, :] // LANES) == coarse, 1.0, 0.0).astype(BF16)
        onehot = jnp.where(fine_ref[:, lat : lat + 1] == lane, 1.0, 0.0).astype(BF16)
        pieces = []
        for ref in (high_ref, low_ref):
            for l in range(levels):
                row = jnp.broadcast_to(ref[l, lat : lat + 1, :], (tiles, lons))
                pieces.append(row.astype(BF16) * mask)
        stacked = jnp.concatenate(pieces, axis=0)
        term = jnp.dot(stacked, onehot, preferred_element_type=F32)
        if lat == 0:
            acc_ref[...] = term
        else:
            acc_ref[...] += term
    size = levels * tiles
    table_ref[...] = acc_ref[pl.ds(0, size), :] + acc_ref[pl.ds(size, size), :]
    device = lax.broadcasted_iota(jnp.int32, (LANES, devices), 1).astype(F32)
    place = lax.broadcasted_iota(jnp.int32, (SLOTS * levels, LANES), 0) // levels
    total = jnp.zeros((SLOTS * levels, devices), F32)
    for t in range(tiles):
        owned = jnp.where(device_ref[:, t : t + 1] == device, 1.0, 0.0).astype(BF16)
        sums = table_ref[pl.ds(t, levels, stride=tiles), :]
        spread = jnp.where(slot_ref[t : t + 1, :] == place, jnp.concatenate([sums] * SLOTS, axis=0), 0.0)
        for piece in split(spread):
            total += jnp.dot(piece, owned, preferred_element_type=F32)
    send_ref[...] = (total * scale).T


def regions(field, ids, fine, device, slot_tiles, levels, devices, scale):
    tiles = slot_tiles.shape[0]
    rows, lons = ids.shape
    whole = (levels, rows, lons)
    return pl.pallas_call(
        functools.partial(region_kernel, scale=scale),
        out_shape=(jax.ShapeDtypeStruct(whole, F32), jax.ShapeDtypeStruct((devices, SLOTS * levels), F32)),
        in_specs=[VMEM] * 5,
        out_specs=(VMEM, VMEM),
        scratch_shapes=[
            pltpu.VMEM(whole, F32),
            pltpu.VMEM(whole, F32),
            pltpu.VMEM((2 * levels * tiles, LANES), F32),
            pltpu.VMEM((levels * tiles, LANES), F32),
        ],
        compiler_params=params(),
        cost_estimate=cost(6),
        name="regions",
    )(field, ids, fine, device, slot_tiles)


def owners_kernel(rows_ref, out_ref):
    devices, lanes = rows_ref.shape
    slots, width = out_ref.shape
    levels = lanes // slots
    groups = width // levels
    total = rows_ref[pl.ds(0, groups), :]
    for first in range(groups, devices, groups):
        total += rows_ref[pl.ds(first, groups), :]
    slot = lax.broadcasted_iota(jnp.int32, (slots, lanes), 0)
    lane = lax.broadcasted_iota(jnp.int32, (slots, lanes), 1)
    mine = slot == lane // levels
    spread = jnp.concatenate([jnp.where(mine, total[j : j + 1], 0.0) for j in range(groups)], axis=1)
    row = lax.broadcasted_iota(jnp.int32, (groups * lanes, width), 0)
    col = lax.broadcasted_iota(jnp.int32, (groups * lanes, width), 1)
    fold = jnp.where(col == row // lanes * levels + row % levels, 1.0, 0.0)
    out_ref[...] = jnp.dot(spread, fold, precision=lax.Precision.HIGHEST, preferred_element_type=F32)


def owners(rows, groups, levels):
    return pl.pallas_call(
        owners_kernel,
        out_shape=jax.ShapeDtypeStruct((SLOTS, groups * levels), F32),
        in_specs=[VMEM],
        out_specs=VMEM,
        compiler_params=params(),
        name="owners",
    )(rows)


def neighbours(up, down):
    count = lax.axis_size("lat")
    forward = [(i, i + 1) for i in range(count - 1)]
    backward = [(target, source) for source, target in forward]
    return lax.ppermute(up, "lat", forward), lax.ppermute(down, "lat", backward)


def local(
    adjoint_in,
    courant_lon,
    codes_lon,
    courant_lat,
    codes_lat,
    courant_lev,
    codes_lev,
    block_inverse,
    block_lower,
    block_upper,
    region_ids,
    owner,
):
    levels_here, bands_here, lon_cells = adjoint_in.shape
    band_count = lax.axis_size("lat")
    group_count = lax.axis_size("lev")
    devices = band_count * group_count
    region_count = owner.shape[0]
    tiles = -(-region_count // LANES)
    tiles = -(-tiles // 8) * 8
    owner_tiles = jnp.pad(owner, (0, tiles * LANES - region_count), constant_values=-1).reshape(tiles, LANES)
    matrix, slot_tiles, fine, device = prep(
        block_inverse, block_lower, block_upper, owner_tiles, region_ids, devices
    )
    last = (lax.axis_index("lat") == band_count - 1).astype(jnp.int32).reshape(1)
    up, down = pack(adjoint_in, courant_lat, codes_lat)
    below, above = neighbours(up, down)
    coefficients = (courant_lat, codes_lat, courant_lon, codes_lon)
    adjoint, swept, edge, lonc = interior(last, (adjoint_in,), coefficients, 0)
    up, down = edges(below, above, edge, lonc, swept)
    below_next, above_next = neighbours(up, down)
    sent, swept = interior(last, (adjoint, up, down), coefficients, group_count)
    sent = edges(below, above, edge, lonc, swept, below_next, above_next, up, down, sent)
    columns = lax.all_to_all(sent, "lev", split_axis=0, concat_axis=0, tiled=True)
    columns = vertical(columns, matrix, courant_lev, codes_lev)
    field = lax.all_to_all(columns, "lev", split_axis=0, concat_axis=0, tiled=True)
    scale = (region_count / (bands_here * band_count * lon_cells)) ** 0.5
    adjoint_out, rows = regions(
        field, region_ids, fine, device, slot_tiles, levels_here, devices, scale
    )
    rows = lax.all_to_all(rows, ("lat", "lev"), split_axis=0, concat_axis=0, tiled=True)
    region_sens = owners(rows, group_count, levels_here)
    return (adjoint_out, region_sens)


def solution(mesh):
    placed = (
        P("lev", "lat", None),
        P("lev", "lat", None),
        P("lev", "lat", None),
        P("lev", "lat", None),
        P("lev", "lat", None),
        P(None, "lat", "lev"),
        P(None, "lat", "lev"),
        P("lat", None, None, None),
        P("lat", None, None, None),
        P("lat", None, None, None),
        P("lat", None),
        P(),
    )
    return jax.shard_map(
        local,
        mesh=mesh,
        in_specs=placed,
        out_specs=(P("lev", "lat", None), P(("lat", "lev"), None)),
        check_vma=False,
    )
```

```python
import functools

import jax
import jax.numpy as jnp
from jax import lax
from jax.experimental import pallas as pl
from jax.experimental.pallas import tpu as pltpu
from jax.sharding import PartitionSpec as P

SUB = 2
SLOTS = 16
LANES = 128
HALF = LANES // 2
LANE_BITS = 7
F32 = jnp.float32
BF16 = jnp.bfloat16
VMEM = pl.BlockSpec(memory_space=pltpu.VMEM)
SMEM = pl.BlockSpec(memory_space=pltpu.SMEM)
HBM = pl.BlockSpec(memory_space=pltpu.HBM)


def params(mib=20):
    return pltpu.CompilerParams(vmem_limit_bytes=mib * 2**20)


def cost(microseconds):
    return pl.CostEstimate(flops=microseconds * 10**9, bytes_accessed=microseconds * 10**6, transcendentals=0)


def flux_parts(courant):
    up = jnp.maximum(courant, 0.0)
    down = jnp.minimum(courant, 0.0)
    half = 0.5 * courant
    return up, down, up * (0.5 - half), down * (0.5 + half)


def slope_parts(codes):
    centred = jnp.where(codes == 3, 0.5, 0.0)
    ahead = jnp.where(codes == 1, 1.0, centred)
    behind = jnp.where(codes == 2, 1.0, centred)
    return ahead, behind


def split(value):
    high = value.astype(BF16)
    low = (value - high.astype(F32)).astype(BF16)
    return high, low


def roll(value, shift, axis):
    return pltpu.roll(value, shift % value.shape[axis], axis)


def wrapped(value, width):
    length = value.shape[1]
    spare = width - length
    first = spare // 2
    return jnp.concatenate([value, value[:, :first], value[:, length - spare + first :]], axis=1)


def sweep_lon(value, up, down, uph, downh, ahead, behind):
    f = roll(value, -1, 1) - value
    s = uph * f - roll(downh * f, 1, 1)
    q = roll(down * f + ahead * s, 1, 1)
    r = roll(behind * s, -1, 1)
    return value + up * f + (behind - ahead) * s + q - r


def lon_parts(courant, codes, width):
    return (*flux_parts(wrapped(courant, width)), *slope_parts(wrapped(codes, width)))


def edge_rows(rows):
    return (0, 1, rows - 2, rows - 1)


def interior_kernel(last_ref, *refs, final):
    if final:
        a_ref, up_ref, down_ref, clat_ref, klat_ref, clon_ref, klon_ref, send_ref, swept_ref, rows_ref = refs
    else:
        a_ref, clat_ref, klat_ref, clon_ref, klon_ref, out_ref, swept_ref, edge_ref, lonc_ref, rows_ref = refs
    levels, rows, lons = a_ref.shape
    width = rows_ref.shape[2]
    half = levels // 2
    last = last_ref[0]
    step = 4 * LANES
    chunks = [(start, min(step, lons - start)) for start in range(0, lons, step)]
    tile = 8

    def level(l, upper):
        for start, size in chunks:
            cols = slice(start, start + size)
            row = lax.broadcasted_iota(jnp.int32, (rows, size), 0)
            lowest, highest = row == 0, row == rows - 1
            a = a_ref[l, :, cols]
            if final:
                a = jnp.where(lowest, down_ref[0, pl.ds(l, 1), cols], a)
                a = jnp.where(row == 1, down_ref[1, pl.ds(l, 1), cols], a)
                a = jnp.where(row == rows - 2, up_ref[1, pl.ds(l, 1), cols], a)
                a = jnp.where(highest, up_ref[0, pl.ds(l, 1), cols], a)
            courant = jnp.where(highest & (last == 1), 0.0, clat_ref[l, :, cols])
            up, down, uph, downh = flux_parts(courant)
            ahead, behind = slope_parts(klat_ref[l, :, cols])
            f = jnp.where(highest, 0.0, roll(a, -1, 0)) - a
            s = uph * f - jnp.where(lowest, 0.0, roll(downh * f, 1, 0))
            q = jnp.where(lowest, 0.0, roll(down * f + ahead * s, 1, 0))
            r = jnp.where(highest, 0.0, roll(behind * s, -1, 0))
            rows_ref[l, :, cols] = a + up * f + (behind - ahead) * s + q - r
        for low in range(0, rows, tile):
            band = slice(low, low + tile)
            value = sweep_lon(
                wrapped(rows_ref[l, band, :lons], width), *lon_parts(clon_ref[l, band, :], klon_ref[l, band, :], width)
            )
            if final:
                parts = send_ref.shape[0]
                share = lons // parts
                for part in range(parts):
                    start = part * share
                    send_ref[part, l, band, :] = value[:, start : start + LANES]
                    rest = value[:, start + LANES : start + share]
                    if upper:
                        send_ref[part, half + l, band, HALF : HALF + share - LANES] = rest
                    else:
                        send_ref[part, levels + l, band, : share - LANES] = rest
            else:
                out_ref[l, band, :] = value[:, :lons]

    def pair(index, carry):
        level(index, False)
        level(index + half, True)
        return carry

    lax.fori_loop(0, half, pair, 0)
    for n, row in enumerate(edge_rows(rows)):
        swept_ref[n] = rows_ref[:, row, :lons]
    if not final:
        high = rows - 1
        courant = jnp.where(last == 1, 0.0, clat_ref[:, high, :])
        up, _, uph, downh = flux_parts(courant)
        ahead, behind = slope_parts(klat_ref[:, high, :])
        ahead0, behind0 = slope_parts(klat_ref[:, 0, :])
        edge_ref[0] = a_ref[:, 0, :]
        edge_ref[1] = a_ref[:, high, :]
        edge_ref[2] = behind0 - ahead0
        edge_ref[3] = ahead0
        edge_ref[4] = up + (behind - ahead) * uph
        edge_ref[5] = behind * uph
        edge_ref[6] = downh
        for n, row in enumerate(edge_rows(rows)):
            for m, part in enumerate(lon_parts(clon_ref[:, row, :], klon_ref[:, row, :], width)):
                lonc_ref[n, m] = part


def interior(last, fields, coefficients, parts):
    levels, rows, lons = fields[0].shape
    width = -(-lons // LANES) * LANES
    final = parts > 0
    whole = (levels, rows, lons)
    swept = jax.ShapeDtypeStruct((4, levels, lons), F32)
    if final:
        out_shape = (jax.ShapeDtypeStruct((parts, levels + levels // 2, rows, LANES), F32), swept)
    else:
        out_shape = (
            jax.ShapeDtypeStruct(whole, F32),
            swept,
            jax.ShapeDtypeStruct((7, levels, lons), F32),
            jax.ShapeDtypeStruct((4, 6, levels, width), F32),
        )
    return pl.pallas_call(
        functools.partial(interior_kernel, final=final),
        out_shape=out_shape,
        in_specs=[SMEM] + [VMEM] * (len(fields) + len(coefficients)),
        out_specs=(VMEM,) * len(out_shape),
        scratch_shapes=[pltpu.VMEM((levels, rows, width), F32)],
        compiler_params=params(),
        cost_estimate=cost(4),
        name="interior",
    )(last, *fields, *coefficients)


def edges_kernel(below_ref, above_ref, edge_ref, lonc_ref, swept_ref, *refs, final):
    width = lonc_ref.shape[3]
    _, levels, lons = swept_ref.shape
    if final:
        below_next, above_next, up_in, down_in, sent_ref, send_ref, main_ref, rest_ref = refs
        row0, row15 = down_in[0], up_in[0]
        am1, am2, a16, a17 = below_next[0], below_next[1], above_next[0], above_next[1]
    else:
        up_ref, down_ref = refs
        row0, row15 = edge_ref[0], edge_ref[1]
        am1, am2, a16, a17 = below_ref[0], below_ref[1], above_ref[0], above_ref[1]
    _, down1, uph1, downh1 = flux_parts(below_ref[2])
    _, _, _, downh2 = flux_parts(below_ref[3])
    ahead1, _ = slope_parts(below_ref[4])
    f1 = row0 - am1
    w = downh1 * f1
    q = down1 * f1 + ahead1 * (uph1 * f1 - downh2 * (am1 - am2))
    _, _, uph16, _ = flux_parts(above_ref[2])
    _, behind16 = slope_parts(above_ref[3])
    r = behind16 * (uph16 * (a17 - a16) - edge_ref[6] * (a16 - row15))
    fixed = (
        swept_ref[0] - edge_ref[2] * w + q,
        swept_ref[1] - edge_ref[3] * w,
        swept_ref[2] - edge_ref[5] * a16,
        swept_ref[3] + edge_ref[4] * a16 - r,
    )
    rows = []
    for n, row in enumerate(fixed):
        rows.append(sweep_lon(wrapped(row, width), *(lonc_ref[n, m] for m in range(6))))
    if final:
        parts, _, count, _ = send_ref.shape
        share = lons // parts
        half = levels // 2
        tile = 8
        sublane = lax.broadcasted_iota(jnp.int32, (tile, LANES), 0)
        lower = lax.broadcasted_iota(jnp.int32, (tile, LANES), 1) < HALF
        first = lax.broadcasted_iota(jnp.int32, (levels, LANES), 0) < half
        blank = jnp.zeros((levels, LANES - (share - LANES)), F32)

        for n, row in enumerate(rows):
            for part in range(parts):
                start = part * share
                main_ref[n, part] = row[:, start : start + LANES]
                rest = jnp.concatenate([row[:, start + LANES : start + share], blank], axis=1)
                rest_ref[n, part] = jnp.where(first, rest, roll(rest, HALF, 1))
        places = edge_rows(count)
        for low in range(0, count, tile):
            band = slice(low, low + tile)
            mine = [(n, place - low) for n, place in enumerate(places) if low <= place < low + tile]
            for part in range(parts):
                for l in range(levels):
                    value = sent_ref[part, l, band, :]
                    for n, place in mine:
                        value = jnp.where(sublane == place, main_ref[n, part, l : l + 1, :], value)
                    send_ref[part, l, band, :] = value
                for l in range(half):
                    value = sent_ref[part, levels + l, band, :]
                    for n, place in mine:
                        both = jnp.where(
                            lower, rest_ref[n, part, l : l + 1, :], rest_ref[n, part, l + half : l + half + 1, :]
                        )
                        value = jnp.where(sublane == place, both, value)
                    send_ref[part, levels + l, band, :] = value
    else:
        down_ref[0], down_ref[1] = rows[0][:, :lons], rows[1][:, :lons]
        up_ref[0], up_ref[1] = rows[3][:, :lons], rows[2][:, :lons]


def edges(below, above, edge, lonc, swept, *more):
    _, levels, lons = swept.shape
    final = len(more) > 0
    args = (below, above, edge, lonc, swept, *more)
    if final:
        out_shape = jax.ShapeDtypeStruct(more[-1].shape, F32)
        scratch = [pltpu.VMEM((4, more[-1].shape[0], levels, LANES), F32)] * 2
    else:
        out_shape = (jax.ShapeDtypeStruct((2, levels, lons), F32),) * 2
        scratch = []
    return pl.pallas_call(
        functools.partial(edges_kernel, final=final),
        out_shape=out_shape,
        in_specs=[VMEM] * len(args),
        out_specs=VMEM if final else (VMEM, VMEM),
        scratch_shapes=scratch,
        compiler_params=params(),
        cost_estimate=cost(1),
        name="edges",
    )(*args)


def pack_kernel(a_in, c_in, k_in, up_ref, down_ref, high_ref, low_ref, sems):
    edge = a_in.shape[1] - 1
    moves = (
        (k_in, edge, high_ref),
        (k_in, 0, low_ref),
        (a_in, edge, up_ref.at[0]),
        (a_in, edge - 1, up_ref.at[1]),
        (c_in, edge, up_ref.at[2]),
        (c_in, edge - 1, up_ref.at[3]),
        (a_in, 0, down_ref.at[0]),
        (a_in, 1, down_ref.at[1]),
        (c_in, 0, down_ref.at[2]),
    )
    copies = [pltpu.make_async_copy(src.at[:, row, :], dst, sems.at[n]) for n, (src, row, dst) in enumerate(moves)]
    for copy in copies:
        copy.start()
    for copy in copies:
        copy.wait()
    up_ref[4] = high_ref[...].astype(F32)
    down_ref[3] = low_ref[...].astype(F32)


def pack(a, clat, klat):
    levels, _, lons = a.shape
    row = (levels, lons)
    return pl.pallas_call(
        pack_kernel,
        out_shape=(jax.ShapeDtypeStruct((5, *row), F32), jax.ShapeDtypeStruct((4, *row), F32)),
        in_specs=[HBM] * 3,
        out_specs=(VMEM, VMEM),
        scratch_shapes=[pltpu.VMEM(row, klat.dtype)] * 2 + [pltpu.SemaphoreType.DMA((9,))],
        compiler_params=params(58),
        cost_estimate=cost(2),
        name="pack",
    )(a, clat, klat)


def prep_kernel(
    inverse_ref, lower_ref, upper_ref, owner_ref, ids_ref, matrix_ref, slot_ref, coarse_ref, fine_ref, device_ref, *, devices, parts
):
    lats, blocks, size, _ = inverse_ref.shape
    group = LANES // size
    levels = blocks * size
    row = lax.broadcasted_iota(jnp.int32, (LANES, LANES), 0)
    col = lax.broadcasted_iota(jnp.int32, (LANES, LANES), 1)
    diagonal = (row // size) == (col // size)
    row_l = lax.broadcasted_iota(jnp.int32, (LANES, levels), 0)
    col_l = lax.broadcasted_iota(jnp.int32, (LANES, levels), 1)

    def times(matrix, vector):
        wide = jnp.concatenate([matrix.reshape(LANES, size)] * group, axis=1)
        wide = jnp.where(diagonal, wide, 0.0)
        return jnp.dot(wide, vector, precision=lax.Precision.HIGHEST, preferred_element_type=F32)

    for first in range(0, lats, group):
        lat = slice(first, first + group)
        solved = []
        for k in range(blocks):
            rhs = jnp.where(col_l == row_l % size + size * k, 1.0, 0.0)
            if k > 0:
                rhs = rhs - times(lower_ref[lat, k - 1], solved[-1])
            solved.append(times(inverse_ref[lat, k], rhs))
        result = [solved[-1]]
        for k in range(blocks - 2, -1, -1):
            result.insert(0, solved[k] - times(upper_ref[lat, k], result[0]))
        for g in range(group):
            dense = jnp.concatenate([block[g * size : (g + 1) * size] for block in result], axis=0)
            high, low = split(dense.T)
            matrix_ref[first + g] = jnp.concatenate([high, low, high], axis=1)

    tiles = owner_ref.shape[0]
    device = lax.broadcasted_iota(jnp.int32, (devices, LANES), 0)
    earlier = jnp.where(row < col, 1.0, 0.0).astype(BF16)
    running = jnp.zeros((devices, 1), F32)
    for t in range(tiles):
        owned = jnp.where(owner_ref[pl.ds(t, 1), :] == device, 1.0, 0.0)
        before = jnp.dot(owned.astype(BF16), earlier, preferred_element_type=F32) + running
        slot_ref[pl.ds(t, 1), :] = jnp.sum(owned * before, axis=0, keepdims=True).astype(jnp.int32)
        running = running + jnp.sum(owned, axis=1, keepdims=True)
    ids = ids_ref[...]
    share = ids.shape[1] // parts
    gap = jnp.full((lats, HALF - (share - LANES)), -1, jnp.int32)
    pieces = [ids[:, part * share : part * share + LANES] for part in range(parts)]
    for part in range(parts):
        pieces += [ids[:, part * share + LANES : (part + 1) * share], gap]
    ids = jnp.concatenate(pieces, axis=1)
    coarse_ref[...] = (ids >> LANE_BITS).astype(F32)
    fine_ref[...] = (ids & (LANES - 1)).astype(F32).T
    device_ref[...] = owner_ref[...].astype(F32).T


def prep(inverse, lower, upper, owner_tiles, ids, devices, parts):
    lats, blocks, size, _ = inverse.shape
    width = parts * (LANES + HALF)
    levels = blocks * size
    return pl.pallas_call(
        functools.partial(prep_kernel, devices=devices, parts=parts),
        out_shape=(
            jax.ShapeDtypeStruct((lats, levels, 3 * levels), BF16),
            jax.ShapeDtypeStruct(owner_tiles.shape, jnp.int32),
            jax.ShapeDtypeStruct((lats, width), F32),
            jax.ShapeDtypeStruct((width, lats), F32),
            jax.ShapeDtypeStruct(owner_tiles.shape[::-1], F32),
        ),
        in_specs=[VMEM] * 5,
        out_specs=(VMEM,) * 5,
        compiler_params=params(),
        cost_estimate=cost(5),
        name="prep",
    )(inverse, lower, upper, owner_tiles, ids)


def unpacked(main, rest, upper, spare):
    if upper:
        rest = roll(rest, HALF, rest.ndim - 1)
    return jnp.concatenate([main, rest[..., :spare]], axis=-1)


def column_rows(ref, part, lat, group, rows):
    half = group // 2
    first = part * (group + half) * rows + lat
    main = ref[pl.ds(first, group, stride=rows), :]
    return main, ref[pl.ds(first + group * rows, half, stride=rows), :]


def vertical_kernel(x_ref, matrix_ref, c_ref, k_ref, out_ref, main_ref, rest_ref, *, group):
    levels, rows, share = c_ref.shape
    half = group // 2
    parts = levels // group
    spare = share - LANES
    for lat in range(rows):
        mains, rests = [], []
        for part in range(parts):
            main, rest = column_rows(x_ref, part, lat, group, rows)
            mains.append(main)
            rests += [rest, roll(rest, HALF, 1)]
        x = jnp.concatenate([jnp.concatenate(mains, axis=0), jnp.concatenate(rests, axis=0)], axis=1)
        high, low = split(x)
        stacked = jnp.concatenate([high, high, low], axis=0)
        y = jnp.dot(matrix_ref[lat], stacked, preferred_element_type=F32)
        main_ref[pl.ds(lat, levels, stride=rows), :] = y[:, :LANES]
        rest_ref[pl.ds(lat, levels, stride=rows), :] = y[:, LANES:]

    def y_at(level):
        band = slice(level * rows, (level + 1) * rows)
        return jnp.concatenate([main_ref[band, :], rest_ref[band, :spare]], axis=1)

    def emit(level, value):
        part, l = level // group, level % group
        first = part * (group + half) * rows
        band = slice(first + l * rows, first + (l + 1) * rows)
        out_ref[band, :] = value[:, :LANES]
        place = first + (group + l % half) * rows
        side = l // half * HALF
        out_ref[place : place + rows, side : side + spare] = value[:, LANES:]

    zero = jnp.zeros((rows, share), F32)
    y = y_at(0)
    prior_w, prior_q, pending = zero, zero, None
    for i in range(levels):
        ahead, behind = slope_parts(k_ref[i])
        if i < levels - 1:
            up, down, uph, downh = flux_parts(c_ref[i])
            y_next = y_at(i + 1)
            f = y_next - y
            s = uph * f - prior_w
            here = y + up * f + prior_q
            prior_w = downh * f
            prior_q = down * f + ahead * s
        else:
            y_next = None
            s = -prior_w
            here = y + prior_q
        here = here + (behind - ahead) * s
        if i > 0:
            emit(i - 1, pending - behind * s)
        pending = here
        y = y_next
    emit(levels - 1, pending)


def vertical(x, matrix, courant, codes, group):
    levels, rows, _ = courant.shape
    return pl.pallas_call(
        functools.partial(vertical_kernel, group=group),
        out_shape=jax.ShapeDtypeStruct(x.shape, F32),
        in_specs=[VMEM] * 4,
        out_specs=VMEM,
        scratch_shapes=[pltpu.VMEM((levels * rows, LANES), F32)] * 2,
        compiler_params=params(),
        cost_estimate=cost(5),
        name="vertical",
    )(x, matrix, courant, codes)


def whole_row(field_ref, l, levels, lons):
    parts = field_ref.shape[0]
    half = levels // 2
    spare = lons // parts - LANES
    return jnp.concatenate(
        [unpacked(field_ref[p, l], field_ref[p, levels + l % half], l // half, spare) for p in range(parts)], axis=1
    )


def rejoin_kernel(field_ref, out_ref):
    levels, _, lons = out_ref.shape
    for l in range(levels):
        out_ref[l] = whole_row(field_ref, l, levels, lons)


def rejoin(field, shape):
    return pl.pallas_call(
        rejoin_kernel,
        out_shape=jax.ShapeDtypeStruct(shape, F32),
        in_specs=[VMEM],
        out_specs=VMEM,
        compiler_params=params(),
        cost_estimate=cost(2),
        name="rejoin",
    )(field)


def region_kernel(field_ref, coarse_ref, fine_ref, device_ref, slot_ref, send_ref, acc_ref, *, levels, scale):
    rows, width = coarse_ref.shape
    parts = width // (LANES + HALF)
    half = levels // 2
    tiles = slot_ref.shape[0]
    devices = send_ref.shape[0]
    lane = lax.broadcasted_iota(jnp.int32, (width, LANES), 1).astype(F32)
    lower = lax.broadcasted_iota(jnp.int32, (half, LANES), 1) < HALF
    for lat in range(rows):
        mains, rests = [], []
        for part in range(parts):
            main, rest = column_rows(field_ref, part, lat, levels, rows)
            mains.append(main)
            rests.append(rest)
        for even, odd in zip(rests[::2], rests[1::2]):
            first = jnp.where(lower, even, roll(odd, HALF, 1))
            second = jnp.where(lower, roll(even, HALF, 1), odd)
            mains.append(jnp.concatenate([first, second], axis=0))
        field = jnp.concatenate(mains, axis=1)
        high = field.astype(BF16).astype(F32)
        both = jnp.concatenate([high, field - high], axis=0)
        coarse = jnp.broadcast_to(coarse_ref[lat : lat + 1, :], both.shape)
        onehot = jnp.where(fine_ref[:, lat : lat + 1] == lane, 1.0, 0.0).astype(BF16)
        stacked = jnp.concatenate([jnp.where(coarse == t, both, 0.0).astype(BF16) for t in range(tiles)], axis=0)
        term = jnp.dot(stacked, onehot, preferred_element_type=F32)
        if lat == 0:
            acc_ref[...] = term
        else:
            acc_ref[...] += term
    device = lax.broadcasted_iota(jnp.int32, (LANES, devices), 1).astype(F32)
    place = lax.broadcasted_iota(jnp.int32, (SLOTS * levels, LANES), 0) // levels
    total = jnp.zeros((SLOTS * levels, devices), F32)
    for t in range(tiles):
        owned = jnp.where(device_ref[:, t : t + 1] == device, 1.0, 0.0).astype(BF16)
        base = 2 * levels * t
        sums = acc_ref[base : base + levels, :] + acc_ref[base + levels : base + 2 * levels, :]
        spread = jnp.where(slot_ref[t : t + 1, :] == place, jnp.concatenate([sums] * SLOTS, axis=0), 0.0)
        for piece in split(spread):
            total += jnp.dot(piece, owned, preferred_element_type=F32)
    send_ref[...] = (total * scale).T


def regions(field, coarse, fine, device, slot_tiles, levels, devices, scale):
    tiles = slot_tiles.shape[0]
    return pl.pallas_call(
        functools.partial(region_kernel, levels=levels, scale=scale),
        out_shape=jax.ShapeDtypeStruct((devices, SLOTS * levels), F32),
        in_specs=[VMEM] * 5,
        out_specs=VMEM,
        scratch_shapes=[pltpu.VMEM((2 * levels * tiles, LANES), F32)],
        compiler_params=params(),
        cost_estimate=cost(6),
        name="regions",
    )(field, coarse, fine, device, slot_tiles)


def owners_kernel(rows_ref, out_ref):
    devices, lanes = rows_ref.shape
    slots, width = out_ref.shape
    levels = lanes // slots
    groups = width // levels
    total = rows_ref[pl.ds(0, groups), :]
    for first in range(groups, devices, groups):
        total += rows_ref[pl.ds(first, groups), :]
    slot = lax.broadcasted_iota(jnp.int32, (slots, lanes), 0)
    lane = lax.broadcasted_iota(jnp.int32, (slots, lanes), 1)
    mine = slot == lane // levels
    spread = jnp.concatenate([jnp.where(mine, total[j : j + 1], 0.0) for j in range(groups)], axis=1)
    row = lax.broadcasted_iota(jnp.int32, (groups * lanes, width), 0)
    col = lax.broadcasted_iota(jnp.int32, (groups * lanes, width), 1)
    fold = jnp.where(col == row // lanes * levels + row % levels, 1.0, 0.0)
    out_ref[...] = jnp.dot(spread, fold, precision=lax.Precision.HIGHEST, preferred_element_type=F32)


def owners(rows, groups, levels):
    return pl.pallas_call(
        owners_kernel,
        out_shape=jax.ShapeDtypeStruct((SLOTS, groups * levels), F32),
        in_specs=[VMEM],
        out_specs=VMEM,
        compiler_params=params(),
        name="owners",
    )(rows)


def neighbours(up, down):
    count = lax.axis_size("lat")
    forward = [(i, i + 1) for i in range(count - 1)]
    backward = [(target, source) for source, target in forward]
    return lax.ppermute(up, "lat", forward), lax.ppermute(down, "lat", backward)


def local(
    adjoint_in,
    courant_lon,
    codes_lon,
    courant_lat,
    codes_lat,
    courant_lev,
    codes_lev,
    block_inverse,
    block_lower,
    block_upper,
    region_ids,
    owner,
):
    levels_here, bands_here, lon_cells = adjoint_in.shape
    band_count = lax.axis_size("lat")
    group_count = lax.axis_size("lev")
    devices = band_count * group_count
    region_count = owner.shape[0]
    tiles = -(-region_count // LANES)
    tiles = -(-tiles // 8) * 8
    owner_tiles = jnp.pad(owner, (0, tiles * LANES - region_count), constant_values=-1).reshape(tiles, LANES)
    matrix, slot_tiles, coarse, fine, device = prep(
        block_inverse, block_lower, block_upper, owner_tiles, region_ids, devices, group_count
    )
    last = (lax.axis_index("lat") == band_count - 1).astype(jnp.int32).reshape(1)
    up, down = pack(adjoint_in, courant_lat, codes_lat)
    below, above = neighbours(up, down)
    coefficients = (courant_lat, codes_lat, courant_lon, codes_lon)
    adjoint, swept, edge, lonc = interior(last, (adjoint_in,), coefficients, 0)
    up, down = edges(below, above, edge, lonc, swept)
    below_next, above_next = neighbours(up, down)
    sent, swept = interior(last, (adjoint, up, down), coefficients, group_count)
    sent = edges(below, above, edge, lonc, swept, below_next, above_next, up, down, sent)
    columns = lax.all_to_all(sent, "lev", split_axis=0, concat_axis=0, tiled=True)
    columns = vertical(columns.reshape(-1, LANES), matrix, courant_lev, codes_lev, levels_here)
    field = lax.all_to_all(columns.reshape(sent.shape), "lev", split_axis=0, concat_axis=0, tiled=True)
    scale = (region_count / (bands_here * band_count * lon_cells)) ** 0.5
    rows = regions(field.reshape(-1, LANES), coarse, fine, device, slot_tiles, levels_here, devices, scale)
    rows = lax.all_to_all(rows, ("lat", "lev"), split_axis=0, concat_axis=0, tiled=True)
    adjoint_out = rejoin(field, adjoint_in.shape)
    region_sens = owners(rows, group_count, levels_here)
    return (adjoint_out, region_sens)


def solution(mesh):
    placed = (
        P("lev", "lat", None),
        P("lev", "lat", None),
        P("lev", "lat", None),
        P("lev", "lat", None),
        P("lev", "lat", None),
        P(None, "lat", "lev"),
        P(None, "lat", "lev"),
        P("lat", None, None, None),
        P("lat", None, None, None),
        P("lat", None, None, None),
        P("lat", None),
        P(),
    )
    return jax.shard_map(
        local,
        mesh=mesh,
        in_specs=placed,
        out_specs=(P("lev", "lat", None), P(("lat", "lev"), None)),
        check_vma=False,
    )
```

```python
import functools

import jax
import jax.numpy as jnp
from jax import lax
from jax.experimental import pallas as pl
from jax.experimental.pallas import tpu as pltpu
from jax.sharding import PartitionSpec as P

SUB = 2
SLOTS = 16
LANES = 128
HALF = LANES // 2
FINE_BITS = 8
FINE = 2**FINE_BITS
F32 = jnp.float32
BF16 = jnp.bfloat16
VMEM = pl.BlockSpec(memory_space=pltpu.VMEM)
SMEM = pl.BlockSpec(memory_space=pltpu.SMEM)
HBM = pl.BlockSpec(memory_space=pltpu.HBM)


def params(mib=20):
    return pltpu.CompilerParams(vmem_limit_bytes=mib * 2**20)


def cost(microseconds):
    return pl.CostEstimate(flops=microseconds * 10**9, bytes_accessed=microseconds * 10**6, transcendentals=0)


def flux_parts(courant):
    up = jnp.maximum(courant, 0.0)
    down = jnp.minimum(courant, 0.0)
    half = 0.5 * courant
    return up, down, up * (0.5 - half), down * (0.5 + half)


def slope_parts(codes):
    centred = jnp.where(codes == 3, 0.5, 0.0)
    ahead = jnp.where(codes == 1, 1.0, centred)
    behind = jnp.where(codes == 2, 1.0, centred)
    return ahead, behind


def split(value):
    high = value.astype(BF16)
    low = (value - high.astype(F32)).astype(BF16)
    return high, low


def roll(value, shift, axis):
    return pltpu.roll(value, shift % value.shape[axis], axis)


def wrapped(value, width):
    length = value.shape[1]
    spare = width - length
    first = spare // 2
    return jnp.concatenate([value, value[:, :first], value[:, length - spare + first :]], axis=1)


def sweep_lon(value, up, down, uph, downh, ahead, behind):
    f = roll(value, -1, 1) - value
    s = uph * f - roll(downh * f, 1, 1)
    q = roll(down * f + ahead * s, 1, 1)
    r = roll(behind * s, -1, 1)
    return value + up * f + (behind - ahead) * s + q - r


def lon_parts(courant, codes, width):
    return (*flux_parts(wrapped(courant, width)), *slope_parts(wrapped(codes, width)))


def edge_rows(rows):
    return (0, 1, rows - 2, rows - 1)


def interior_kernel(last_ref, *refs, final):
    if final:
        a_ref, up_ref, down_ref, clat_ref, klat_ref, clon_ref, klon_ref, send_ref, swept_ref, rows_ref = refs
    else:
        a_ref, clat_ref, klat_ref, clon_ref, klon_ref, out_ref, swept_ref, edge_ref, lonc_ref, rows_ref = refs
    levels, rows, lons = a_ref.shape
    width = rows_ref.shape[2]
    half = levels // 2
    last = last_ref[0]
    step = 4 * LANES
    chunks = [(start, min(step, lons - start)) for start in range(0, lons, step)]
    tile = 8

    def level(l, upper):
        for start, size in chunks:
            cols = slice(start, start + size)
            row = lax.broadcasted_iota(jnp.int32, (rows, size), 0)
            lowest, highest = row == 0, row == rows - 1
            a = a_ref[l, :, cols]
            if final:
                a = jnp.where(lowest, down_ref[0, pl.ds(l, 1), cols], a)
                a = jnp.where(row == 1, down_ref[1, pl.ds(l, 1), cols], a)
                a = jnp.where(row == rows - 2, up_ref[1, pl.ds(l, 1), cols], a)
                a = jnp.where(highest, up_ref[0, pl.ds(l, 1), cols], a)
            courant = jnp.where(highest & (last == 1), 0.0, clat_ref[l, :, cols])
            up, down, uph, downh = flux_parts(courant)
            ahead, behind = slope_parts(klat_ref[l, :, cols])
            f = jnp.where(highest, 0.0, roll(a, -1, 0)) - a
            s = uph * f - jnp.where(lowest, 0.0, roll(downh * f, 1, 0))
            q = jnp.where(lowest, 0.0, roll(down * f + ahead * s, 1, 0))
            r = jnp.where(highest, 0.0, roll(behind * s, -1, 0))
            rows_ref[l, :, cols] = a + up * f + (behind - ahead) * s + q - r
        for low in range(0, rows, tile):
            band = slice(low, low + tile)
            value = sweep_lon(
                wrapped(rows_ref[l, band, :lons], width), *lon_parts(clon_ref[l, band, :], klon_ref[l, band, :], width)
            )
            if final:
                parts = send_ref.shape[0]
                share = lons // parts
                for part in range(parts):
                    start = part * share
                    send_ref[part, l, band, :] = value[:, start : start + LANES]
                    rest = value[:, start + LANES : start + share]
                    if upper:
                        send_ref[part, half + l, band, HALF : HALF + share - LANES] = rest
                    else:
                        send_ref[part, levels + l, band, : share - LANES] = rest
            else:
                out_ref[l, band, :] = value[:, :lons]

    def pair(index, carry):
        level(index, False)
        level(index + half, True)
        return carry

    lax.fori_loop(0, half, pair, 0)
    for n, row in enumerate(edge_rows(rows)):
        swept_ref[n] = rows_ref[:, row, :lons]
    if not final:
        high = rows - 1
        courant = jnp.where(last == 1, 0.0, clat_ref[:, high, :])
        up, _, uph, downh = flux_parts(courant)
        ahead, behind = slope_parts(klat_ref[:, high, :])
        ahead0, behind0 = slope_parts(klat_ref[:, 0, :])
        edge_ref[0] = a_ref[:, 0, :]
        edge_ref[1] = a_ref[:, high, :]
        edge_ref[2] = behind0 - ahead0
        edge_ref[3] = ahead0
        edge_ref[4] = up + (behind - ahead) * uph
        edge_ref[5] = behind * uph
        edge_ref[6] = downh
        for n, row in enumerate(edge_rows(rows)):
            for m, part in enumerate(lon_parts(clon_ref[:, row, :], klon_ref[:, row, :], width)):
                lonc_ref[n, m] = part


def interior(last, fields, coefficients, parts):
    levels, rows, lons = fields[0].shape
    width = -(-lons // LANES) * LANES
    final = parts > 0
    whole = (levels, rows, lons)
    swept = jax.ShapeDtypeStruct((4, levels, lons), F32)
    if final:
        out_shape = (jax.ShapeDtypeStruct((parts, levels + levels // 2, rows, LANES), F32), swept)
    else:
        out_shape = (
            jax.ShapeDtypeStruct(whole, F32),
            swept,
            jax.ShapeDtypeStruct((7, levels, lons), F32),
            jax.ShapeDtypeStruct((4, 6, levels, width), F32),
        )
    return pl.pallas_call(
        functools.partial(interior_kernel, final=final),
        out_shape=out_shape,
        in_specs=[SMEM] + [VMEM] * (len(fields) + len(coefficients)),
        out_specs=(VMEM,) * len(out_shape),
        scratch_shapes=[pltpu.VMEM((levels, rows, width), F32)],
        compiler_params=params(),
        cost_estimate=cost(4),
        name="interior",
    )(last, *fields, *coefficients)


def edges_kernel(below_ref, above_ref, edge_ref, lonc_ref, swept_ref, *refs, final):
    width = lonc_ref.shape[3]
    _, levels, lons = swept_ref.shape
    if final:
        below_next, above_next, up_in, down_in, sent_ref, send_ref, main_ref, rest_ref = refs
        row0, row15 = down_in[0], up_in[0]
        am1, am2, a16, a17 = below_next[0], below_next[1], above_next[0], above_next[1]
    else:
        up_ref, down_ref = refs
        row0, row15 = edge_ref[0], edge_ref[1]
        am1, am2, a16, a17 = below_ref[0], below_ref[1], above_ref[0], above_ref[1]
    _, down1, uph1, downh1 = flux_parts(below_ref[2])
    _, _, _, downh2 = flux_parts(below_ref[3])
    ahead1, _ = slope_parts(below_ref[4])
    f1 = row0 - am1
    w = downh1 * f1
    q = down1 * f1 + ahead1 * (uph1 * f1 - downh2 * (am1 - am2))
    _, _, uph16, _ = flux_parts(above_ref[2])
    _, behind16 = slope_parts(above_ref[3])
    r = behind16 * (uph16 * (a17 - a16) - edge_ref[6] * (a16 - row15))
    fixed = (
        swept_ref[0] - edge_ref[2] * w + q,
        swept_ref[1] - edge_ref[3] * w,
        swept_ref[2] - edge_ref[5] * a16,
        swept_ref[3] + edge_ref[4] * a16 - r,
    )
    rows = []
    for n, row in enumerate(fixed):
        rows.append(sweep_lon(wrapped(row, width), *(lonc_ref[n, m] for m in range(6))))
    if final:
        parts, _, count, _ = send_ref.shape
        share = lons // parts
        half = levels // 2
        tile = 8
        sublane = lax.broadcasted_iota(jnp.int32, (tile, LANES), 0)
        lower = lax.broadcasted_iota(jnp.int32, (tile, LANES), 1) < HALF
        first = lax.broadcasted_iota(jnp.int32, (levels, LANES), 0) < half
        blank = jnp.zeros((levels, LANES - (share - LANES)), F32)

        for n, row in enumerate(rows):
            for part in range(parts):
                start = part * share
                main_ref[n, part] = row[:, start : start + LANES]
                rest = jnp.concatenate([row[:, start + LANES : start + share], blank], axis=1)
                rest_ref[n, part] = jnp.where(first, rest, roll(rest, HALF, 1))
        places = edge_rows(count)
        for low in range(0, count, tile):
            band = slice(low, low + tile)
            mine = [(n, place - low) for n, place in enumerate(places) if low <= place < low + tile]
            for part in range(parts):
                for l in range(levels):
                    value = sent_ref[part, l, band, :]
                    for n, place in mine:
                        value = jnp.where(sublane == place, main_ref[n, part, l : l + 1, :], value)
                    send_ref[part, l, band, :] = value
                for l in range(half):
                    value = sent_ref[part, levels + l, band, :]
                    for n, place in mine:
                        both = jnp.where(
                            lower, rest_ref[n, part, l : l + 1, :], rest_ref[n, part, l + half : l + half + 1, :]
                        )
                        value = jnp.where(sublane == place, both, value)
                    send_ref[part, levels + l, band, :] = value
    else:
        down_ref[0], down_ref[1] = rows[0][:, :lons], rows[1][:, :lons]
        up_ref[0], up_ref[1] = rows[3][:, :lons], rows[2][:, :lons]


def edges(below, above, edge, lonc, swept, *more):
    _, levels, lons = swept.shape
    final = len(more) > 0
    args = (below, above, edge, lonc, swept, *more)
    if final:
        out_shape = jax.ShapeDtypeStruct(more[-1].shape, F32)
        scratch = [pltpu.VMEM((4, more[-1].shape[0], levels, LANES), F32)] * 2
    else:
        out_shape = (jax.ShapeDtypeStruct((2, levels, lons), F32),) * 2
        scratch = []
    return pl.pallas_call(
        functools.partial(edges_kernel, final=final),
        out_shape=out_shape,
        in_specs=[VMEM] * len(args),
        out_specs=VMEM if final else (VMEM, VMEM),
        scratch_shapes=scratch,
        compiler_params=params(),
        cost_estimate=cost(1),
        name="edges",
    )(*args)


def pack_kernel(a_in, c_in, k_in, up_ref, down_ref, high_ref, low_ref, sems):
    edge = a_in.shape[1] - 1
    moves = (
        (k_in, edge, high_ref),
        (k_in, 0, low_ref),
        (a_in, edge, up_ref.at[0]),
        (a_in, edge - 1, up_ref.at[1]),
        (c_in, edge, up_ref.at[2]),
        (c_in, edge - 1, up_ref.at[3]),
        (a_in, 0, down_ref.at[0]),
        (a_in, 1, down_ref.at[1]),
        (c_in, 0, down_ref.at[2]),
    )
    copies = [pltpu.make_async_copy(src.at[:, row, :], dst, sems.at[n]) for n, (src, row, dst) in enumerate(moves)]
    for copy in copies:
        copy.start()
    for copy in copies:
        copy.wait()
    up_ref[4] = high_ref[...].astype(F32)
    down_ref[3] = low_ref[...].astype(F32)


def pack(a, clat, klat):
    levels, _, lons = a.shape
    row = (levels, lons)
    return pl.pallas_call(
        pack_kernel,
        out_shape=(jax.ShapeDtypeStruct((5, *row), F32), jax.ShapeDtypeStruct((4, *row), F32)),
        in_specs=[HBM] * 3,
        out_specs=(VMEM, VMEM),
        scratch_shapes=[pltpu.VMEM(row, klat.dtype)] * 2 + [pltpu.SemaphoreType.DMA((9,))],
        compiler_params=params(58),
        cost_estimate=cost(2),
        name="pack",
    )(a, clat, klat)


def prep_kernel(
    inverse_ref, lower_ref, upper_ref, owner_ref, ids_ref, matrix_ref, slot_ref, coarse_ref, fine_ref, device_ref, *, devices, parts
):
    lats, blocks, size, _ = inverse_ref.shape
    group = LANES // size
    levels = blocks * size
    row = lax.broadcasted_iota(jnp.int32, (LANES, LANES), 0)
    col = lax.broadcasted_iota(jnp.int32, (LANES, LANES), 1)
    diagonal = (row // size) == (col // size)
    row_l = lax.broadcasted_iota(jnp.int32, (LANES, levels), 0)
    col_l = lax.broadcasted_iota(jnp.int32, (LANES, levels), 1)

    def times(matrix, vector):
        wide = jnp.concatenate([matrix.reshape(LANES, size)] * group, axis=1)
        wide = jnp.where(diagonal, wide, 0.0)
        return jnp.dot(wide, vector, precision=lax.Precision.HIGHEST, preferred_element_type=F32)

    for first in range(0, lats, group):
        lat = slice(first, first + group)
        solved = []
        for k in range(blocks):
            rhs = jnp.where(col_l == row_l % size + size * k, 1.0, 0.0)
            if k > 0:
                rhs = rhs - times(lower_ref[lat, k - 1], solved[-1])
            solved.append(times(inverse_ref[lat, k], rhs))
        result = [solved[-1]]
        for k in range(blocks - 2, -1, -1):
            result.insert(0, solved[k] - times(upper_ref[lat, k], result[0]))
        for g in range(group):
            dense = jnp.concatenate([block[g * size : (g + 1) * size] for block in result], axis=0)
            high, low = split(dense.T)
            matrix_ref[first + g] = jnp.concatenate([high, low, high], axis=1)

    tiles = owner_ref.shape[0]
    device = lax.broadcasted_iota(jnp.int32, (devices, FINE), 0)
    row_f = lax.broadcasted_iota(jnp.int32, (FINE, FINE), 0)
    col_f = lax.broadcasted_iota(jnp.int32, (FINE, FINE), 1)
    earlier = jnp.where(row_f < col_f, 1.0, 0.0).astype(BF16)
    running = jnp.zeros((devices, 1), F32)
    for t in range(tiles):
        owned = jnp.where(owner_ref[pl.ds(t, 1), :] == device, 1.0, 0.0)
        before = jnp.dot(owned.astype(BF16), earlier, preferred_element_type=F32) + running
        slot_ref[pl.ds(t, 1), :] = jnp.sum(owned * before, axis=0, keepdims=True).astype(jnp.int32)
        running = running + jnp.sum(owned, axis=1, keepdims=True)
    ids = ids_ref[...]
    share = ids.shape[1] // parts
    gap = jnp.full((lats, HALF - (share - LANES)), -1, jnp.int32)
    pieces = [ids[:, part * share : part * share + LANES] for part in range(parts)]
    for part in range(parts):
        pieces += [ids[:, part * share + LANES : (part + 1) * share], gap]
    ids = jnp.concatenate(pieces, axis=1)
    coarse_ref[...] = (ids >> FINE_BITS).astype(F32)
    fine_ref[...] = (ids & (FINE - 1)).astype(F32).T
    device_ref[...] = owner_ref[...].astype(F32).T


def prep(inverse, lower, upper, owner_tiles, ids, devices, parts):
    lats, blocks, size, _ = inverse.shape
    width = parts * (LANES + HALF)
    levels = blocks * size
    return pl.pallas_call(
        functools.partial(prep_kernel, devices=devices, parts=parts),
        out_shape=(
            jax.ShapeDtypeStruct((lats, levels, 3 * levels), BF16),
            jax.ShapeDtypeStruct(owner_tiles.shape, jnp.int32),
            jax.ShapeDtypeStruct((lats, width), F32),
            jax.ShapeDtypeStruct((width, lats), F32),
            jax.ShapeDtypeStruct(owner_tiles.shape[::-1], F32),
        ),
        in_specs=[VMEM] * 5,
        out_specs=(VMEM,) * 5,
        compiler_params=params(),
        cost_estimate=cost(5),
        name="prep",
    )(inverse, lower, upper, owner_tiles, ids)


def unpacked(main, rest, upper, spare):
    if upper:
        rest = roll(rest, HALF, rest.ndim - 1)
    return jnp.concatenate([main, rest[..., :spare]], axis=-1)


def column_rows(ref, part, lat, group, rows):
    half = group // 2
    first = part * (group + half) * rows + lat
    main = ref[pl.ds(first, group, stride=rows), :]
    return main, ref[pl.ds(first + group * rows, half, stride=rows), :]


def vertical_kernel(x_ref, matrix_ref, c_ref, k_ref, out_ref, main_ref, rest_ref, *, group):
    levels, rows, share = c_ref.shape
    half = group // 2
    parts = levels // group
    spare = share - LANES
    for lat in range(rows):
        mains, rests = [], []
        for part in range(parts):
            main, rest = column_rows(x_ref, part, lat, group, rows)
            mains.append(main)
            rests += [rest, roll(rest, HALF, 1)]
        x = jnp.concatenate([jnp.concatenate(mains, axis=0), jnp.concatenate(rests, axis=0)], axis=1)
        high, low = split(x)
        stacked = jnp.concatenate([high, high, low], axis=0)
        y = jnp.dot(matrix_ref[lat], stacked, preferred_element_type=F32)
        main_ref[pl.ds(lat, levels, stride=rows), :] = y[:, :LANES]
        rest_ref[pl.ds(lat, levels, stride=rows), :] = y[:, LANES:]

    def y_at(level):
        band = slice(level * rows, (level + 1) * rows)
        return jnp.concatenate([main_ref[band, :], rest_ref[band, :spare]], axis=1)

    def emit(level, value):
        part, l = level // group, level % group
        first = part * (group + half) * rows
        band = slice(first + l * rows, first + (l + 1) * rows)
        out_ref[band, :] = value[:, :LANES]
        place = first + (group + l % half) * rows
        side = l // half * HALF
        out_ref[place : place + rows, side : side + spare] = value[:, LANES:]

    zero = jnp.zeros((rows, share), F32)
    y = y_at(0)
    prior_w, prior_q, pending = zero, zero, None
    for i in range(levels):
        ahead, behind = slope_parts(k_ref[i])
        if i < levels - 1:
            up, down, uph, downh = flux_parts(c_ref[i])
            y_next = y_at(i + 1)
            f = y_next - y
            s = uph * f - prior_w
            here = y + up * f + prior_q
            prior_w = downh * f
            prior_q = down * f + ahead * s
        else:
            y_next = None
            s = -prior_w
            here = y + prior_q
        here = here + (behind - ahead) * s
        if i > 0:
            emit(i - 1, pending - behind * s)
        pending = here
        y = y_next
    emit(levels - 1, pending)


def vertical(x, matrix, courant, codes, group):
    levels, rows, _ = courant.shape
    return pl.pallas_call(
        functools.partial(vertical_kernel, group=group),
        out_shape=jax.ShapeDtypeStruct(x.shape, F32),
        in_specs=[VMEM] * 4,
        out_specs=VMEM,
        scratch_shapes=[pltpu.VMEM((levels * rows, LANES), F32)] * 2,
        compiler_params=params(),
        cost_estimate=cost(5),
        name="vertical",
    )(x, matrix, courant, codes)


def whole_row(field_ref, l, levels, lons):
    parts = field_ref.shape[0]
    half = levels // 2
    spare = lons // parts - LANES
    return jnp.concatenate(
        [unpacked(field_ref[p, l], field_ref[p, levels + l % half], l // half, spare) for p in range(parts)], axis=1
    )


def rejoin_kernel(field_ref, out_ref):
    levels, _, lons = out_ref.shape
    for l in range(levels):
        out_ref[l] = whole_row(field_ref, l, levels, lons)


def rejoin(field, shape):
    return pl.pallas_call(
        rejoin_kernel,
        out_shape=jax.ShapeDtypeStruct(shape, F32),
        in_specs=[VMEM],
        out_specs=VMEM,
        compiler_params=params(),
        cost_estimate=cost(2),
        name="rejoin",
    )(field)


def region_kernel(field_ref, coarse_ref, fine_ref, device_ref, slot_ref, send_ref, acc_ref, *, levels, scale):
    rows, width = coarse_ref.shape
    parts = width // (LANES + HALF)
    half = levels // 2
    tiles = slot_ref.shape[0]
    devices = send_ref.shape[0]
    lane = lax.broadcasted_iota(jnp.int32, (width, FINE), 1).astype(F32)
    lower = lax.broadcasted_iota(jnp.int32, (half, LANES), 1) < HALF
    for lat in range(rows):
        mains, rests = [], []
        for part in range(parts):
            main, rest = column_rows(field_ref, part, lat, levels, rows)
            mains.append(main)
            rests.append(rest)
        for even, odd in zip(rests[::2], rests[1::2]):
            first = jnp.where(lower, even, roll(odd, HALF, 1))
            second = jnp.where(lower, roll(even, HALF, 1), odd)
            mains.append(jnp.concatenate([first, second], axis=0))
        field = jnp.concatenate(mains, axis=1)
        high = field.astype(BF16).astype(F32)
        both = jnp.concatenate([high, field - high], axis=0)
        coarse = jnp.broadcast_to(coarse_ref[lat : lat + 1, :], both.shape)
        onehot = jnp.where(fine_ref[:, lat : lat + 1] == lane, 1.0, 0.0).astype(BF16)
        stacked = jnp.concatenate([jnp.where(coarse == t, both, 0.0).astype(BF16) for t in range(tiles)], axis=0)
        term = jnp.dot(stacked, onehot, preferred_element_type=F32)
        if lat == 0:
            acc_ref[...] = term
        else:
            acc_ref[...] += term
    device = lax.broadcasted_iota(jnp.int32, (FINE, devices), 1).astype(F32)
    place = lax.broadcasted_iota(jnp.int32, (SLOTS * levels, FINE), 0) // levels
    total = jnp.zeros((SLOTS * levels, devices), F32)
    for t in range(tiles):
        owned = jnp.where(device_ref[:, t : t + 1] == device, 1.0, 0.0).astype(BF16)
        base = 2 * levels * t
        sums = acc_ref[base : base + levels, :] + acc_ref[base + levels : base + 2 * levels, :]
        spread = jnp.where(slot_ref[t : t + 1, :] == place, jnp.concatenate([sums] * SLOTS, axis=0), 0.0)
        for piece in split(spread):
            total += jnp.dot(piece, owned, preferred_element_type=F32)
    send_ref[...] = (total * scale).T


def regions(field, coarse, fine, device, slot_tiles, levels, devices, scale):
    tiles = slot_tiles.shape[0]
    return pl.pallas_call(
        functools.partial(region_kernel, levels=levels, scale=scale),
        out_shape=jax.ShapeDtypeStruct((devices, SLOTS * levels), F32),
        in_specs=[VMEM] * 5,
        out_specs=VMEM,
        scratch_shapes=[pltpu.VMEM((2 * levels * tiles, FINE), F32)],
        compiler_params=params(),
        cost_estimate=cost(6),
        name="regions",
    )(field, coarse, fine, device, slot_tiles)


def owners_kernel(rows_ref, out_ref):
    devices, lanes = rows_ref.shape
    slots, width = out_ref.shape
    levels = lanes // slots
    groups = width // levels
    total = rows_ref[pl.ds(0, groups), :]
    for first in range(groups, devices, groups):
        total += rows_ref[pl.ds(first, groups), :]
    slot = lax.broadcasted_iota(jnp.int32, (slots, lanes), 0)
    lane = lax.broadcasted_iota(jnp.int32, (slots, lanes), 1)
    mine = slot == lane // levels
    spread = jnp.concatenate([jnp.where(mine, total[j : j + 1], 0.0) for j in range(groups)], axis=1)
    row = lax.broadcasted_iota(jnp.int32, (groups * lanes, width), 0)
    col = lax.broadcasted_iota(jnp.int32, (groups * lanes, width), 1)
    fold = jnp.where(col == row // lanes * levels + row % levels, 1.0, 0.0)
    out_ref[...] = jnp.dot(spread, fold, precision=lax.Precision.HIGHEST, preferred_element_type=F32)


def owners(rows, groups, levels):
    return pl.pallas_call(
        owners_kernel,
        out_shape=jax.ShapeDtypeStruct((SLOTS, groups * levels), F32),
        in_specs=[VMEM],
        out_specs=VMEM,
        compiler_params=params(),
        name="owners",
    )(rows)


def neighbours(up, down):
    count = lax.axis_size("lat")
    forward = [(i, i + 1) for i in range(count - 1)]
    backward = [(target, source) for source, target in forward]
    return lax.ppermute(up, "lat", forward), lax.ppermute(down, "lat", backward)


def local(
    adjoint_in,
    courant_lon,
    codes_lon,
    courant_lat,
    codes_lat,
    courant_lev,
    codes_lev,
    block_inverse,
    block_lower,
    block_upper,
    region_ids,
    owner,
):
    levels_here, bands_here, lon_cells = adjoint_in.shape
    band_count = lax.axis_size("lat")
    group_count = lax.axis_size("lev")
    devices = band_count * group_count
    region_count = owner.shape[0]
    tiles = -(-region_count // (8 * FINE)) * 8
    owner_tiles = jnp.pad(owner, (0, tiles * FINE - region_count), constant_values=-1).reshape(tiles, FINE)
    matrix, slot_tiles, coarse, fine, device = prep(
        block_inverse, block_lower, block_upper, owner_tiles, region_ids, devices, group_count
    )
    last = (lax.axis_index("lat") == band_count - 1).astype(jnp.int32).reshape(1)
    up, down = pack(adjoint_in, courant_lat, codes_lat)
    below, above = neighbours(up, down)
    coefficients = (courant_lat, codes_lat, courant_lon, codes_lon)
    adjoint, swept, edge, lonc = interior(last, (adjoint_in,), coefficients, 0)
    up, down = edges(below, above, edge, lonc, swept)
    below_next, above_next = neighbours(up, down)
    sent, swept = interior(last, (adjoint, up, down), coefficients, group_count)
    sent = edges(below, above, edge, lonc, swept, below_next, above_next, up, down, sent)
    columns = lax.all_to_all(sent, "lev", split_axis=0, concat_axis=0, tiled=True)
    columns = vertical(columns.reshape(-1, LANES), matrix, courant_lev, codes_lev, levels_here)
    field = lax.all_to_all(columns.reshape(sent.shape), "lev", split_axis=0, concat_axis=0, tiled=True)
    scale = (region_count / (bands_here * band_count * lon_cells)) ** 0.5
    rows = regions(field.reshape(-1, LANES), coarse, fine, device, slot_tiles, levels_here, devices, scale)
    rows = lax.all_to_all(rows, ("lat", "lev"), split_axis=0, concat_axis=0, tiled=True)
    adjoint_out = rejoin(field, adjoint_in.shape)
    region_sens = owners(rows, group_count, levels_here)
    return (adjoint_out, region_sens)


def solution(mesh):
    placed = (
        P("lev", "lat", None),
        P("lev", "lat", None),
        P("lev", "lat", None),
        P("lev", "lat", None),
        P("lev", "lat", None),
        P(None, "lat", "lev"),
        P(None, "lat", "lev"),
        P("lat", None, None, None),
        P("lat", None, None, None),
        P("lat", None, None, None),
        P("lat", None),
        P(),
    )
    return jax.shard_map(
        local,
        mesh=mesh,
        in_specs=placed,
        out_specs=(P("lev", "lat", None), P(("lat", "lev"), None)),
        check_vma=False,
    )
```

```python
import functools

import jax
import jax.numpy as jnp
from jax import lax
from jax.experimental import pallas as pl
from jax.experimental.pallas import tpu as pltpu
from jax.sharding import PartitionSpec as P

SUB = 2
SLOTS = 16
LANES = 128
HALF = LANES // 2
FINE_BITS = 8
FINE = 2**FINE_BITS
F32 = jnp.float32
BF16 = jnp.bfloat16
VMEM = pl.BlockSpec(memory_space=pltpu.VMEM)
SMEM = pl.BlockSpec(memory_space=pltpu.SMEM)
HBM = pl.BlockSpec(memory_space=pltpu.HBM)


def params(mib=20):
    return pltpu.CompilerParams(vmem_limit_bytes=mib * 2**20)


def cost(microseconds):
    return pl.CostEstimate(flops=microseconds * 10**9, bytes_accessed=microseconds * 10**6, transcendentals=0)


def flux_parts(courant):
    up = jnp.maximum(courant, 0.0)
    down = jnp.minimum(courant, 0.0)
    half = 0.5 * courant
    return up, down, up * (0.5 - half), down * (0.5 + half)


def slope_parts(codes):
    centred = jnp.where(codes == 3, 0.5, 0.0)
    ahead = jnp.where(codes == 1, 1.0, centred)
    behind = jnp.where(codes == 2, 1.0, centred)
    return ahead, behind


def split(value):
    high = value.astype(BF16)
    low = (value - high.astype(F32)).astype(BF16)
    return high, low


def roll(value, shift, axis):
    return pltpu.roll(value, shift % value.shape[axis], axis)


def wrapped(value, width):
    length = value.shape[1]
    spare = width - length
    first = spare // 2
    return jnp.concatenate([value, value[:, :first], value[:, length - spare + first :]], axis=1)


def sweep_lon(value, up, down, uph, downh, ahead, behind):
    f = roll(value, -1, 1) - value
    s = uph * f - roll(downh * f, 1, 1)
    q = roll(down * f + ahead * s, 1, 1)
    r = roll(behind * s, -1, 1)
    return value + up * f + (behind - ahead) * s + q - r


def lon_parts(courant, codes, width):
    return (*flux_parts(wrapped(courant, width)), *slope_parts(wrapped(codes, width)))


def edge_rows(rows):
    return (0, 1, rows - 2, rows - 1)


def sweep_lat(a, courant, codes):
    rows, size = a.shape
    row = lax.broadcasted_iota(jnp.int32, (rows, size), 0)
    lowest, highest = row == 0, row == rows - 1
    up, down, uph, downh = flux_parts(courant)
    ahead, behind = slope_parts(codes)
    f = jnp.where(highest, 0.0, roll(a, -1, 0)) - a
    s = uph * f - jnp.where(lowest, 0.0, roll(downh * f, 1, 0))
    q = jnp.where(lowest, 0.0, roll(down * f + ahead * s, 1, 0))
    r = jnp.where(highest, 0.0, roll(behind * s, -1, 0))
    return a + up * f + (behind - ahead) * s + q - r


def lane_chunks(lons):
    step = 4 * LANES
    return [slice(start, min(start + step, lons)) for start in range(0, lons, step)]


def walled(last, courant):
    rows = courant.shape[0]
    row = lax.broadcasted_iota(jnp.int32, courant.shape, 0)
    return jnp.where((row == rows - 1) & (last == 1), 0.0, courant)


def first_lat_kernel(last_ref, a_ref, clat_ref, klat_ref, rows_ref, swept_ref, edge_ref):
    levels, rows, lons = a_ref.shape
    last = last_ref[0]

    def level(l, carry):
        for cols in lane_chunks(lons):
            rows_ref[l, :, cols] = sweep_lat(
                a_ref[l, :, cols], walled(last, clat_ref[l, :, cols]), klat_ref[l, :, cols]
            )
        return carry

    lax.fori_loop(0, levels, level, 0)
    for n, row in enumerate(edge_rows(rows)):
        swept_ref[n] = rows_ref[:, row, :]
    high = rows - 1
    courant = jnp.where(last == 1, 0.0, clat_ref[:, high, :])
    up, _, uph, downh = flux_parts(courant)
    ahead, behind = slope_parts(klat_ref[:, high, :])
    ahead0, behind0 = slope_parts(klat_ref[:, 0, :])
    edge_ref[0] = a_ref[:, 0, :]
    edge_ref[1] = a_ref[:, high, :]
    edge_ref[2] = behind0 - ahead0
    edge_ref[3] = ahead0
    edge_ref[4] = up + (behind - ahead) * uph
    edge_ref[5] = behind * uph
    edge_ref[6] = downh


def first_lat(last, a, clat, klat):
    levels, rows, lons = a.shape
    return pl.pallas_call(
        first_lat_kernel,
        out_shape=(
            jax.ShapeDtypeStruct(a.shape, F32),
            jax.ShapeDtypeStruct((4, levels, lons), F32),
            jax.ShapeDtypeStruct((7, levels, lons), F32),
        ),
        in_specs=[SMEM] + [VMEM] * 3,
        out_specs=(VMEM,) * 3,
        compiler_params=params(),
        cost_estimate=cost(2),
        name="first_lat",
    )(last, a, clat, klat)


def first_lon_kernel(rows_ref, clon_ref, klon_ref, out_ref, lonc_ref):
    levels, rows, lons = rows_ref.shape
    width = lonc_ref.shape[3]
    tile = 8

    def level(l, carry):
        for low in range(0, rows, tile):
            band = slice(low, low + tile)
            value = sweep_lon(
                wrapped(rows_ref[l, band, :], width), *lon_parts(clon_ref[l, band, :], klon_ref[l, band, :], width)
            )
            out_ref[l, band, :] = value[:, :lons]
        return carry

    lax.fori_loop(0, levels, level, 0)
    for n, row in enumerate(edge_rows(rows)):
        for m, part in enumerate(lon_parts(clon_ref[:, row, :], klon_ref[:, row, :], width)):
            lonc_ref[n, m] = part


def first_lon(swept, clon, klon):
    levels, _, lons = swept.shape
    width = -(-lons // LANES) * LANES
    return pl.pallas_call(
        first_lon_kernel,
        out_shape=(jax.ShapeDtypeStruct(swept.shape, F32), jax.ShapeDtypeStruct((4, 6, levels, width), F32)),
        in_specs=[VMEM] * 3,
        out_specs=(VMEM,) * 2,
        compiler_params=params(),
        cost_estimate=cost(2),
        name="first_lon",
    )(swept, clon, klon)


def interior_kernel(
    last_ref, a_ref, up_ref, down_ref, clat_ref, klat_ref, clon_ref, klon_ref, send_ref, swept_ref, rows_ref
):
    levels, rows, lons = a_ref.shape
    width = rows_ref.shape[2]
    half = levels // 2
    last = last_ref[0]
    tile = 8

    def level(l, upper):
        for cols in lane_chunks(lons):
            a = a_ref[l, :, cols]
            row = lax.broadcasted_iota(jnp.int32, a.shape, 0)
            a = jnp.where(row == 0, down_ref[0, pl.ds(l, 1), cols], a)
            a = jnp.where(row == 1, down_ref[1, pl.ds(l, 1), cols], a)
            a = jnp.where(row == rows - 2, up_ref[1, pl.ds(l, 1), cols], a)
            a = jnp.where(row == rows - 1, up_ref[0, pl.ds(l, 1), cols], a)
            rows_ref[l, :, cols] = sweep_lat(a, walled(last, clat_ref[l, :, cols]), klat_ref[l, :, cols])
        parts = send_ref.shape[0]
        share = lons // parts
        for low in range(0, rows, tile):
            band = slice(low, low + tile)
            value = sweep_lon(
                wrapped(rows_ref[l, band, :lons], width), *lon_parts(clon_ref[l, band, :], klon_ref[l, band, :], width)
            )
            for part in range(parts):
                start = part * share
                send_ref[part, l, band, :] = value[:, start : start + LANES]
                rest = value[:, start + LANES : start + share]
                if upper:
                    send_ref[part, half + l, band, HALF : HALF + share - LANES] = rest
                else:
                    send_ref[part, levels + l, band, : share - LANES] = rest

    def pair(index, carry):
        level(index, False)
        level(index + half, True)
        return carry

    lax.fori_loop(0, half, pair, 0)
    for n, row in enumerate(edge_rows(rows)):
        swept_ref[n] = rows_ref[:, row, :lons]


def interior(last, fields, coefficients, parts):
    levels, rows, lons = fields[0].shape
    width = -(-lons // LANES) * LANES
    return pl.pallas_call(
        interior_kernel,
        out_shape=(
            jax.ShapeDtypeStruct((parts, levels + levels // 2, rows, LANES), F32),
            jax.ShapeDtypeStruct((4, levels, lons), F32),
        ),
        in_specs=[SMEM] + [VMEM] * (len(fields) + len(coefficients)),
        out_specs=(VMEM,) * 2,
        scratch_shapes=[pltpu.VMEM((levels, rows, width), F32)],
        compiler_params=params(),
        cost_estimate=cost(4),
        name="interior",
    )(last, *fields, *coefficients)


def edges_kernel(below_ref, above_ref, edge_ref, lonc_ref, swept_ref, *refs, final):
    width = lonc_ref.shape[3]
    _, levels, lons = swept_ref.shape
    if final:
        below_next, above_next, up_in, down_in, sent_ref, send_ref, main_ref, rest_ref = refs
        row0, row15 = down_in[0], up_in[0]
        am1, am2, a16, a17 = below_next[0], below_next[1], above_next[0], above_next[1]
    else:
        up_ref, down_ref = refs
        row0, row15 = edge_ref[0], edge_ref[1]
        am1, am2, a16, a17 = below_ref[0], below_ref[1], above_ref[0], above_ref[1]
    _, down1, uph1, downh1 = flux_parts(below_ref[2])
    _, _, _, downh2 = flux_parts(below_ref[3])
    ahead1, _ = slope_parts(below_ref[4])
    f1 = row0 - am1
    w = downh1 * f1
    q = down1 * f1 + ahead1 * (uph1 * f1 - downh2 * (am1 - am2))
    _, _, uph16, _ = flux_parts(above_ref[2])
    _, behind16 = slope_parts(above_ref[3])
    r = behind16 * (uph16 * (a17 - a16) - edge_ref[6] * (a16 - row15))
    fixed = (
        swept_ref[0] - edge_ref[2] * w + q,
        swept_ref[1] - edge_ref[3] * w,
        swept_ref[2] - edge_ref[5] * a16,
        swept_ref[3] + edge_ref[4] * a16 - r,
    )
    rows = []
    for n, row in enumerate(fixed):
        rows.append(sweep_lon(wrapped(row, width), *(lonc_ref[n, m] for m in range(6))))
    if final:
        parts, _, count, _ = send_ref.shape
        share = lons // parts
        half = levels // 2
        tile = 8
        sublane = lax.broadcasted_iota(jnp.int32, (tile, LANES), 0)
        lower = lax.broadcasted_iota(jnp.int32, (tile, LANES), 1) < HALF
        first = lax.broadcasted_iota(jnp.int32, (levels, LANES), 0) < half
        blank = jnp.zeros((levels, LANES - (share - LANES)), F32)

        for n, row in enumerate(rows):
            for part in range(parts):
                start = part * share
                main_ref[n, part] = row[:, start : start + LANES]
                rest = jnp.concatenate([row[:, start + LANES : start + share], blank], axis=1)
                rest_ref[n, part] = jnp.where(first, rest, roll(rest, HALF, 1))
        places = edge_rows(count)
        for low in range(0, count, tile):
            band = slice(low, low + tile)
            mine = [(n, place - low) for n, place in enumerate(places) if low <= place < low + tile]
            for part in range(parts):
                for l in range(levels):
                    value = sent_ref[part, l, band, :]
                    for n, place in mine:
                        value = jnp.where(sublane == place, main_ref[n, part, l : l + 1, :], value)
                    send_ref[part, l, band, :] = value
                for l in range(half):
                    value = sent_ref[part, levels + l, band, :]
                    for n, place in mine:
                        both = jnp.where(
                            lower, rest_ref[n, part, l : l + 1, :], rest_ref[n, part, l + half : l + half + 1, :]
                        )
                        value = jnp.where(sublane == place, both, value)
                    send_ref[part, levels + l, band, :] = value
    else:
        down_ref[0], down_ref[1] = rows[0][:, :lons], rows[1][:, :lons]
        up_ref[0], up_ref[1] = rows[3][:, :lons], rows[2][:, :lons]


def edges(below, above, edge, lonc, swept, *more):
    _, levels, lons = swept.shape
    final = len(more) > 0
    args = (below, above, edge, lonc, swept, *more)
    if final:
        out_shape = jax.ShapeDtypeStruct(more[-1].shape, F32)
        scratch = [pltpu.VMEM((4, more[-1].shape[0], levels, LANES), F32)] * 2
    else:
        out_shape = (jax.ShapeDtypeStruct((2, levels, lons), F32),) * 2
        scratch = []
    return pl.pallas_call(
        functools.partial(edges_kernel, final=final),
        out_shape=out_shape,
        in_specs=[VMEM] * len(args),
        out_specs=VMEM if final else (VMEM, VMEM),
        scratch_shapes=scratch,
        compiler_params=params(),
        cost_estimate=cost(1),
        name="edges",
    )(*args)


def pack_kernel(a_in, c_in, k_in, up_ref, down_ref, high_ref, low_ref, sems):
    edge = a_in.shape[1] - 1
    moves = (
        (k_in, edge, high_ref),
        (k_in, 0, low_ref),
        (a_in, edge, up_ref.at[0]),
        (a_in, edge - 1, up_ref.at[1]),
        (c_in, edge, up_ref.at[2]),
        (c_in, edge - 1, up_ref.at[3]),
        (a_in, 0, down_ref.at[0]),
        (a_in, 1, down_ref.at[1]),
        (c_in, 0, down_ref.at[2]),
    )
    copies = [pltpu.make_async_copy(src.at[:, row, :], dst, sems.at[n]) for n, (src, row, dst) in enumerate(moves)]
    for copy in copies:
        copy.start()
    for copy in copies:
        copy.wait()
    up_ref[4] = high_ref[...].astype(F32)
    down_ref[3] = low_ref[...].astype(F32)


def pack(a, clat, klat):
    levels, _, lons = a.shape
    row = (levels, lons)
    return pl.pallas_call(
        pack_kernel,
        out_shape=(jax.ShapeDtypeStruct((5, *row), F32), jax.ShapeDtypeStruct((4, *row), F32)),
        in_specs=[HBM] * 3,
        out_specs=(VMEM, VMEM),
        scratch_shapes=[pltpu.VMEM(row, klat.dtype)] * 2 + [pltpu.SemaphoreType.DMA((9,))],
        compiler_params=params(58),
        cost_estimate=cost(2),
        name="pack",
    )(a, clat, klat)


def prep_kernel(
    inverse_ref, lower_ref, upper_ref, owner_ref, ids_ref, matrix_ref, slot_ref, coarse_ref, fine_ref, device_ref, *, devices, parts
):
    lats, blocks, size, _ = inverse_ref.shape
    group = LANES // size
    levels = blocks * size
    row = lax.broadcasted_iota(jnp.int32, (LANES, LANES), 0)
    col = lax.broadcasted_iota(jnp.int32, (LANES, LANES), 1)
    diagonal = (row // size) == (col // size)
    row_l = lax.broadcasted_iota(jnp.int32, (LANES, levels), 0)
    col_l = lax.broadcasted_iota(jnp.int32, (LANES, levels), 1)

    def times(matrix, vector):
        wide = jnp.concatenate([matrix.reshape(LANES, size)] * group, axis=1)
        wide = jnp.where(diagonal, wide, 0.0)
        return jnp.dot(wide, vector, precision=lax.Precision.HIGHEST, preferred_element_type=F32)

    for first in range(0, lats, group):
        lat = slice(first, first + group)
        solved = []
        for k in range(blocks):
            rhs = jnp.where(col_l == row_l % size + size * k, 1.0, 0.0)
            if k > 0:
                rhs = rhs - times(lower_ref[lat, k - 1], solved[-1])
            solved.append(times(inverse_ref[lat, k], rhs))
        result = [solved[-1]]
        for k in range(blocks - 2, -1, -1):
            result.insert(0, solved[k] - times(upper_ref[lat, k], result[0]))
        for g in range(group):
            dense = jnp.concatenate([block[g * size : (g + 1) * size] for block in result], axis=0)
            high, low = split(dense.T)
            matrix_ref[first + g] = jnp.concatenate([high, low, high], axis=1)

    tiles = owner_ref.shape[0]
    device = lax.broadcasted_iota(jnp.int32, (devices, FINE), 0)
    row_f = lax.broadcasted_iota(jnp.int32, (FINE, FINE), 0)
    col_f = lax.broadcasted_iota(jnp.int32, (FINE, FINE), 1)
    earlier = jnp.where(row_f < col_f, 1.0, 0.0).astype(BF16)
    running = jnp.zeros((devices, 1), F32)
    for t in range(tiles):
        owned = jnp.where(owner_ref[pl.ds(t, 1), :] == device, 1.0, 0.0)
        before = jnp.dot(owned.astype(BF16), earlier, preferred_element_type=F32) + running
        slot_ref[pl.ds(t, 1), :] = jnp.sum(owned * before, axis=0, keepdims=True).astype(jnp.int32)
        running = running + jnp.sum(owned, axis=1, keepdims=True)
    ids = ids_ref[...]
    share = ids.shape[1] // parts
    gap = jnp.full((lats, HALF - (share - LANES)), -1, jnp.int32)
    pieces = [ids[:, part * share : part * share + LANES] for part in range(parts)]
    for part in range(parts):
        pieces += [ids[:, part * share + LANES : (part + 1) * share], gap]
    ids = jnp.concatenate(pieces, axis=1)
    coarse_ref[...] = (ids >> FINE_BITS).astype(F32)
    fine_ref[...] = (ids & (FINE - 1)).astype(F32).T
    device_ref[...] = owner_ref[...].astype(F32).T


def prep(inverse, lower, upper, owner_tiles, ids, devices, parts):
    lats, blocks, size, _ = inverse.shape
    width = parts * (LANES + HALF)
    levels = blocks * size
    return pl.pallas_call(
        functools.partial(prep_kernel, devices=devices, parts=parts),
        out_shape=(
            jax.ShapeDtypeStruct((lats, levels, 3 * levels), BF16),
            jax.ShapeDtypeStruct(owner_tiles.shape, jnp.int32),
            jax.ShapeDtypeStruct((lats, width), F32),
            jax.ShapeDtypeStruct((width, lats), F32),
            jax.ShapeDtypeStruct(owner_tiles.shape[::-1], F32),
        ),
        in_specs=[VMEM] * 5,
        out_specs=(VMEM,) * 5,
        compiler_params=params(),
        cost_estimate=cost(5),
        name="prep",
    )(inverse, lower, upper, owner_tiles, ids)


def unpacked(main, rest, upper, spare):
    if upper:
        rest = roll(rest, HALF, rest.ndim - 1)
    return jnp.concatenate([main, rest[..., :spare]], axis=-1)


def column_rows(ref, part, lat, group, rows):
    half = group // 2
    first = part * (group + half) * rows + lat
    main = ref[pl.ds(first, group, stride=rows), :]
    return main, ref[pl.ds(first + group * rows, half, stride=rows), :]


def vertical_kernel(x_ref, matrix_ref, c_ref, k_ref, out_ref, main_ref, rest_ref, *, group):
    levels, rows, share = c_ref.shape
    half = group // 2
    parts = levels // group
    spare = share - LANES
    for lat in range(rows):
        mains, rests = [], []
        for part in range(parts):
            main, rest = column_rows(x_ref, part, lat, group, rows)
            mains.append(main)
            rests += [rest, roll(rest, HALF, 1)]
        x = jnp.concatenate([jnp.concatenate(mains, axis=0), jnp.concatenate(rests, axis=0)], axis=1)
        high, low = split(x)
        stacked = jnp.concatenate([high, high, low], axis=0)
        y = jnp.dot(matrix_ref[lat], stacked, preferred_element_type=F32)
        main_ref[pl.ds(lat, levels, stride=rows), :] = y[:, :LANES]
        rest_ref[pl.ds(lat, levels, stride=rows), :] = y[:, LANES:]

    def y_at(level):
        band = slice(level * rows, (level + 1) * rows)
        return jnp.concatenate([main_ref[band, :], rest_ref[band, :spare]], axis=1)

    def emit(level, value):
        part, l = level // group, level % group
        first = part * (group + half) * rows
        band = slice(first + l * rows, first + (l + 1) * rows)
        out_ref[band, :] = value[:, :LANES]
        place = first + (group + l % half) * rows
        side = l // half * HALF
        out_ref[place : place + rows, side : side + spare] = value[:, LANES:]

    zero = jnp.zeros((rows, share), F32)
    y = y_at(0)
    prior_w, prior_q, pending = zero, zero, None
    for i in range(levels):
        ahead, behind = slope_parts(k_ref[i])
        if i < levels - 1:
            up, down, uph, downh = flux_parts(c_ref[i])
            y_next = y_at(i + 1)
            f = y_next - y
            s = uph * f - prior_w
            here = y + up * f + prior_q
            prior_w = downh * f
            prior_q = down * f + ahead * s
        else:
            y_next = None
            s = -prior_w
            here = y + prior_q
        here = here + (behind - ahead) * s
        if i > 0:
            emit(i - 1, pending - behind * s)
        pending = here
        y = y_next
    emit(levels - 1, pending)


def vertical(x, matrix, courant, codes, group):
    levels, rows, _ = courant.shape
    return pl.pallas_call(
        functools.partial(vertical_kernel, group=group),
        out_shape=jax.ShapeDtypeStruct(x.shape, F32),
        in_specs=[VMEM] * 4,
        out_specs=VMEM,
        scratch_shapes=[pltpu.VMEM((levels * rows, LANES), F32)] * 2,
        compiler_params=params(),
        cost_estimate=cost(5),
        name="vertical",
    )(x, matrix, courant, codes)


def whole_row(field_ref, l, levels, lons):
    parts = field_ref.shape[0]
    half = levels // 2
    spare = lons // parts - LANES
    return jnp.concatenate(
        [unpacked(field_ref[p, l], field_ref[p, levels + l % half], l // half, spare) for p in range(parts)], axis=1
    )


def rejoin_kernel(field_ref, out_ref):
    levels, _, lons = out_ref.shape
    for l in range(levels):
        out_ref[l] = whole_row(field_ref, l, levels, lons)


def rejoin(field, shape):
    return pl.pallas_call(
        rejoin_kernel,
        out_shape=jax.ShapeDtypeStruct(shape, F32),
        in_specs=[VMEM],
        out_specs=VMEM,
        compiler_params=params(),
        cost_estimate=cost(2),
        name="rejoin",
    )(field)


def region_kernel(field_ref, coarse_ref, fine_ref, device_ref, slot_ref, send_ref, acc_ref, *, levels, scale):
    rows, width = coarse_ref.shape
    parts = width // (LANES + HALF)
    half = levels // 2
    tiles = slot_ref.shape[0]
    devices = send_ref.shape[0]
    lane = lax.broadcasted_iota(jnp.int32, (width, FINE), 1).astype(F32)
    lower = lax.broadcasted_iota(jnp.int32, (half, LANES), 1) < HALF
    for lat in range(rows):
        mains, rests = [], []
        for part in range(parts):
            main, rest = column_rows(field_ref, part, lat, levels, rows)
            mains.append(main)
            rests.append(rest)
        for even, odd in zip(rests[::2], rests[1::2]):
            first = jnp.where(lower, even, roll(odd, HALF, 1))
            second = jnp.where(lower, roll(even, HALF, 1), odd)
            mains.append(jnp.concatenate([first, second], axis=0))
        field = jnp.concatenate(mains, axis=1)
        high = field.astype(BF16).astype(F32)
        both = jnp.concatenate([high, field - high], axis=0)
        coarse = jnp.broadcast_to(coarse_ref[lat : lat + 1, :], both.shape)
        onehot = jnp.where(fine_ref[:, lat : lat + 1] == lane, 1.0, 0.0).astype(BF16)
        stacked = jnp.concatenate([jnp.where(coarse == t, both, 0.0).astype(BF16) for t in range(tiles)], axis=0)
        term = jnp.dot(stacked, onehot, preferred_element_type=F32)
        if lat == 0:
            acc_ref[...] = term
        else:
            acc_ref[...] += term
    device = lax.broadcasted_iota(jnp.int32, (FINE, devices), 1).astype(F32)
    place = lax.broadcasted_iota(jnp.int32, (SLOTS * levels, FINE), 0) // levels
    total = jnp.zeros((SLOTS * levels, devices), F32)
    for t in range(tiles):
        owned = jnp.where(device_ref[:, t : t + 1] == device, 1.0, 0.0).astype(BF16)
        base = 2 * levels * t
        sums = acc_ref[base : base + levels, :] + acc_ref[base + levels : base + 2 * levels, :]
        spread = jnp.where(slot_ref[t : t + 1, :] == place, jnp.concatenate([sums] * SLOTS, axis=0), 0.0)
        for piece in split(spread):
            total += jnp.dot(piece, owned, preferred_element_type=F32)
    send_ref[...] = (total * scale).T


def regions(field, coarse, fine, device, slot_tiles, levels, devices, scale):
    tiles = slot_tiles.shape[0]
    return pl.pallas_call(
        functools.partial(region_kernel, levels=levels, scale=scale),
        out_shape=jax.ShapeDtypeStruct((devices, SLOTS * levels), F32),
        in_specs=[VMEM] * 5,
        out_specs=VMEM,
        scratch_shapes=[pltpu.VMEM((2 * levels * tiles, FINE), F32)],
        compiler_params=params(),
        cost_estimate=cost(6),
        name="regions",
    )(field, coarse, fine, device, slot_tiles)


def owners_kernel(rows_ref, out_ref):
    devices, lanes = rows_ref.shape
    slots, width = out_ref.shape
    levels = lanes // slots
    groups = width // levels
    total = rows_ref[pl.ds(0, groups), :]
    for first in range(groups, devices, groups):
        total += rows_ref[pl.ds(first, groups), :]
    slot = lax.broadcasted_iota(jnp.int32, (slots, lanes), 0)
    lane = lax.broadcasted_iota(jnp.int32, (slots, lanes), 1)
    mine = slot == lane // levels
    spread = jnp.concatenate([jnp.where(mine, total[j : j + 1], 0.0) for j in range(groups)], axis=1)
    row = lax.broadcasted_iota(jnp.int32, (groups * lanes, width), 0)
    col = lax.broadcasted_iota(jnp.int32, (groups * lanes, width), 1)
    fold = jnp.where(col == row // lanes * levels + row % levels, 1.0, 0.0)
    out_ref[...] = jnp.dot(spread, fold, precision=lax.Precision.HIGHEST, preferred_element_type=F32)


def owners(rows, groups, levels):
    return pl.pallas_call(
        owners_kernel,
        out_shape=jax.ShapeDtypeStruct((SLOTS, groups * levels), F32),
        in_specs=[VMEM],
        out_specs=VMEM,
        compiler_params=params(),
        name="owners",
    )(rows)


def neighbours(up, down):
    count = lax.axis_size("lat")
    forward = [(i, i + 1) for i in range(count - 1)]
    backward = [(target, source) for source, target in forward]
    return lax.ppermute(up, "lat", forward), lax.ppermute(down, "lat", backward)


def local(
    adjoint_in,
    courant_lon,
    codes_lon,
    courant_lat,
    codes_lat,
    courant_lev,
    codes_lev,
    block_inverse,
    block_lower,
    block_upper,
    region_ids,
    owner,
):
    levels_here, bands_here, lon_cells = adjoint_in.shape
    band_count = lax.axis_size("lat")
    group_count = lax.axis_size("lev")
    devices = band_count * group_count
    region_count = owner.shape[0]
    tiles = -(-region_count // (8 * FINE)) * 8
    owner_tiles = jnp.pad(owner, (0, tiles * FINE - region_count), constant_values=-1).reshape(tiles, FINE)
    matrix, slot_tiles, coarse, fine, device = prep(
        block_inverse, block_lower, block_upper, owner_tiles, region_ids, devices, group_count
    )
    last = (lax.axis_index("lat") == band_count - 1).astype(jnp.int32).reshape(1)
    up, down = pack(adjoint_in, courant_lat, codes_lat)
    below, above = neighbours(up, down)
    coefficients = (courant_lat, codes_lat, courant_lon, codes_lon)
    partial, swept, edge = first_lat(last, adjoint_in, courant_lat, codes_lat)
    adjoint, lonc = first_lon(partial, courant_lon, codes_lon)
    up, down = edges(below, above, edge, lonc, swept)
    below_next, above_next = neighbours(up, down)
    sent, swept = interior(last, (adjoint, up, down), coefficients, group_count)
    sent = edges(below, above, edge, lonc, swept, below_next, above_next, up, down, sent)
    columns = lax.all_to_all(sent, "lev", split_axis=0, concat_axis=0, tiled=True)
    columns = vertical(columns.reshape(-1, LANES), matrix, courant_lev, codes_lev, levels_here)
    field = lax.all_to_all(columns.reshape(sent.shape), "lev", split_axis=0, concat_axis=0, tiled=True)
    scale = (region_count / (bands_here * band_count * lon_cells)) ** 0.5
    rows = regions(field.reshape(-1, LANES), coarse, fine, device, slot_tiles, levels_here, devices, scale)
    rows = lax.all_to_all(rows, ("lat", "lev"), split_axis=0, concat_axis=0, tiled=True)
    adjoint_out = rejoin(field, adjoint_in.shape)
    region_sens = owners(rows, group_count, levels_here)
    return (adjoint_out, region_sens)


def solution(mesh):
    placed = (
        P("lev", "lat", None),
        P("lev", "lat", None),
        P("lev", "lat", None),
        P("lev", "lat", None),
        P("lev", "lat", None),
        P(None, "lat", "lev"),
        P(None, "lat", "lev"),
        P("lat", None, None, None),
        P("lat", None, None, None),
        P("lat", None, None, None),
        P("lat", None),
        P(),
    )
    return jax.shard_map(
        local,
        mesh=mesh,
        in_specs=placed,
        out_specs=(P("lev", "lat", None), P(("lat", "lev"), None)),
        check_vma=False,
    )
```

```python
import functools

import jax
import jax.numpy as jnp
from jax import lax
from jax.experimental import pallas as pl
from jax.experimental.pallas import tpu as pltpu
from jax.sharding import PartitionSpec as P

SUB = 2
SLOTS = 16
LANES = 128
HALF = LANES // 2
FINE_BITS = 8
FINE = 2**FINE_BITS
F32 = jnp.float32
BF16 = jnp.bfloat16
VMEM = pl.BlockSpec(memory_space=pltpu.VMEM)
SMEM = pl.BlockSpec(memory_space=pltpu.SMEM)
HBM = pl.BlockSpec(memory_space=pltpu.HBM)


def params(mib=20):
    return pltpu.CompilerParams(vmem_limit_bytes=mib * 2**20)


def cost(microseconds):
    return pl.CostEstimate(flops=microseconds * 10**9, bytes_accessed=microseconds * 10**6, transcendentals=0)


def flux_parts(courant):
    up = jnp.maximum(courant, 0.0)
    down = jnp.minimum(courant, 0.0)
    half = 0.5 * courant
    return up, down, up * (0.5 - half), down * (0.5 + half)


def slope_parts(codes):
    centred = jnp.where(codes == 3, 0.5, 0.0)
    ahead = jnp.where(codes == 1, 1.0, centred)
    behind = jnp.where(codes == 2, 1.0, centred)
    return ahead, behind


def split(value):
    high = value.astype(BF16)
    low = (value - high.astype(F32)).astype(BF16)
    return high, low


def roll(value, shift, axis):
    return pltpu.roll(value, shift % value.shape[axis], axis)


def wrapped(value, width):
    length = value.shape[1]
    spare = width - length
    first = spare // 2
    return jnp.concatenate([value, value[:, :first], value[:, length - spare + first :]], axis=1)


def sweep_lon(value, up, down, uph, downh, ahead, behind):
    f = roll(value, -1, 1) - value
    s = uph * f - roll(downh * f, 1, 1)
    q = roll(down * f + ahead * s, 1, 1)
    r = roll(behind * s, -1, 1)
    return value + up * f + (behind - ahead) * s + q - r


def lon_parts(courant, codes, width):
    return (*flux_parts(wrapped(courant, width)), *slope_parts(wrapped(codes, width)))


def edge_rows(rows):
    return (0, 1, rows - 2, rows - 1)


def sweep_lat(a, courant, codes):
    rows, size = a.shape
    row = lax.broadcasted_iota(jnp.int32, (rows, size), 0)
    lowest, highest = row == 0, row == rows - 1
    up, down, uph, downh = flux_parts(courant)
    ahead, behind = slope_parts(codes)
    f = jnp.where(highest, 0.0, roll(a, -1, 0)) - a
    s = uph * f - jnp.where(lowest, 0.0, roll(downh * f, 1, 0))
    q = jnp.where(lowest, 0.0, roll(down * f + ahead * s, 1, 0))
    r = jnp.where(highest, 0.0, roll(behind * s, -1, 0))
    return a + up * f + (behind - ahead) * s + q - r


def lane_chunks(lons):
    step = 4 * LANES
    return [slice(start, min(start + step, lons)) for start in range(0, lons, step)]


def walled(last, courant):
    rows = courant.shape[0]
    row = lax.broadcasted_iota(jnp.int32, courant.shape, 0)
    return jnp.where((row == rows - 1) & (last == 1), 0.0, courant)


def first_lat_kernel(last_ref, a_ref, clat_ref, klat_ref, rows_ref, swept_ref, edge_ref):
    levels, rows, lons = a_ref.shape
    last = last_ref[0]

    def level(l, carry):
        for cols in lane_chunks(lons):
            rows_ref[l, :, cols] = sweep_lat(
                a_ref[l, :, cols], walled(last, clat_ref[l, :, cols]), klat_ref[l, :, cols]
            )
        return carry

    lax.fori_loop(0, levels, level, 0)
    for n, row in enumerate(edge_rows(rows)):
        swept_ref[n] = rows_ref[:, row, :]
    high = rows - 1
    courant = jnp.where(last == 1, 0.0, clat_ref[:, high, :])
    up, _, uph, downh = flux_parts(courant)
    ahead, behind = slope_parts(klat_ref[:, high, :])
    ahead0, behind0 = slope_parts(klat_ref[:, 0, :])
    edge_ref[0] = a_ref[:, 0, :]
    edge_ref[1] = a_ref[:, high, :]
    edge_ref[2] = behind0 - ahead0
    edge_ref[3] = ahead0
    edge_ref[4] = up + (behind - ahead) * uph
    edge_ref[5] = behind * uph
    edge_ref[6] = downh


def first_lat(last, a, clat, klat):
    levels, rows, lons = a.shape
    return pl.pallas_call(
        first_lat_kernel,
        out_shape=(
            jax.ShapeDtypeStruct(a.shape, F32),
            jax.ShapeDtypeStruct((4, levels, lons), F32),
            jax.ShapeDtypeStruct((7, levels, lons), F32),
        ),
        in_specs=[SMEM] + [VMEM] * 3,
        out_specs=(VMEM,) * 3,
        compiler_params=params(),
        cost_estimate=cost(2),
        name="first_lat",
    )(last, a, clat, klat)


def first_lon_kernel(rows_ref, clon_ref, klon_ref, out_ref, lonc_ref):
    levels, rows, lons = rows_ref.shape
    width = lonc_ref.shape[3]
    tile = 8

    def level(l, carry):
        for low in range(0, rows, tile):
            band = slice(low, low + tile)
            value = sweep_lon(
                wrapped(rows_ref[l, band, :], width), *lon_parts(clon_ref[l, band, :], klon_ref[l, band, :], width)
            )
            out_ref[l, band, :] = value[:, :lons]
        return carry

    lax.fori_loop(0, levels, level, 0)
    for n, row in enumerate(edge_rows(rows)):
        for m, part in enumerate(lon_parts(clon_ref[:, row, :], klon_ref[:, row, :], width)):
            lonc_ref[n, m] = part


def first_lon(swept, clon, klon):
    levels, _, lons = swept.shape
    width = -(-lons // LANES) * LANES
    return pl.pallas_call(
        first_lon_kernel,
        out_shape=(jax.ShapeDtypeStruct(swept.shape, F32), jax.ShapeDtypeStruct((4, 6, levels, width), F32)),
        in_specs=[VMEM] * 3,
        out_specs=(VMEM,) * 2,
        compiler_params=params(),
        cost_estimate=cost(2),
        name="first_lon",
    )(swept, clon, klon)


def interior_kernel(
    last_ref, a_ref, up_ref, down_ref, clat_ref, klat_ref, clon_ref, klon_ref, send_ref, swept_ref, rows_ref
):
    levels, rows, lons = a_ref.shape
    width = rows_ref.shape[2]
    half = levels // 2
    last = last_ref[0]
    tile = 8

    def level(l, upper):
        for cols in lane_chunks(lons):
            a = a_ref[l, :, cols]
            row = lax.broadcasted_iota(jnp.int32, a.shape, 0)
            a = jnp.where(row == 0, down_ref[0, pl.ds(l, 1), cols], a)
            a = jnp.where(row == 1, down_ref[1, pl.ds(l, 1), cols], a)
            a = jnp.where(row == rows - 2, up_ref[1, pl.ds(l, 1), cols], a)
            a = jnp.where(row == rows - 1, up_ref[0, pl.ds(l, 1), cols], a)
            rows_ref[l, :, cols] = sweep_lat(a, walled(last, clat_ref[l, :, cols]), klat_ref[l, :, cols])
        parts = send_ref.shape[0]
        share = lons // parts
        for low in range(0, rows, tile):
            band = slice(low, low + tile)
            value = sweep_lon(
                wrapped(rows_ref[l, band, :lons], width), *lon_parts(clon_ref[l, band, :], klon_ref[l, band, :], width)
            )
            for part in range(parts):
                start = part * share
                send_ref[part, l, band, :] = value[:, start : start + LANES]
                rest = value[:, start + LANES : start + share]
                if upper:
                    send_ref[part, half + l, band, HALF : HALF + share - LANES] = rest
                else:
                    send_ref[part, levels + l, band, : share - LANES] = rest

    def pair(index, carry):
        level(index, False)
        level(index + half, True)
        return carry

    lax.fori_loop(0, half, pair, 0)
    for n, row in enumerate(edge_rows(rows)):
        swept_ref[n] = rows_ref[:, row, :lons]


def interior(last, fields, coefficients, parts):
    levels, rows, lons = fields[0].shape
    width = -(-lons // LANES) * LANES
    return pl.pallas_call(
        interior_kernel,
        out_shape=(
            jax.ShapeDtypeStruct((parts, levels + levels // 2, rows, LANES), F32),
            jax.ShapeDtypeStruct((4, levels, lons), F32),
        ),
        in_specs=[SMEM] + [VMEM] * (len(fields) + len(coefficients)),
        out_specs=(VMEM,) * 2,
        scratch_shapes=[pltpu.VMEM((levels, rows, width), F32)],
        compiler_params=params(),
        cost_estimate=cost(4),
        name="interior",
    )(last, *fields, *coefficients)


def edges_kernel(below_ref, above_ref, edge_ref, lonc_ref, swept_ref, *refs, final):
    width = lonc_ref.shape[3]
    _, levels, lons = swept_ref.shape
    if final:
        below_next, above_next, up_in, down_in, sent_ref, send_ref, main_ref, rest_ref = refs
        row0, row15 = down_in[0], up_in[0]
        am1, am2, a16, a17 = below_next[0], below_next[1], above_next[0], above_next[1]
    else:
        up_ref, down_ref = refs
        row0, row15 = edge_ref[0], edge_ref[1]
        am1, am2, a16, a17 = below_ref[0], below_ref[1], above_ref[0], above_ref[1]
    _, down1, uph1, downh1 = flux_parts(below_ref[2])
    _, _, _, downh2 = flux_parts(below_ref[3])
    ahead1, _ = slope_parts(below_ref[4])
    f1 = row0 - am1
    w = downh1 * f1
    q = down1 * f1 + ahead1 * (uph1 * f1 - downh2 * (am1 - am2))
    _, _, uph16, _ = flux_parts(above_ref[2])
    _, behind16 = slope_parts(above_ref[3])
    r = behind16 * (uph16 * (a17 - a16) - edge_ref[6] * (a16 - row15))
    fixed = (
        swept_ref[0] - edge_ref[2] * w + q,
        swept_ref[1] - edge_ref[3] * w,
        swept_ref[2] - edge_ref[5] * a16,
        swept_ref[3] + edge_ref[4] * a16 - r,
    )
    rows = []
    for n, row in enumerate(fixed):
        rows.append(sweep_lon(wrapped(row, width), *(lonc_ref[n, m] for m in range(6))))
    if final:
        parts, _, count, _ = send_ref.shape
        share = lons // parts
        half = levels // 2
        tile = 8
        sublane = lax.broadcasted_iota(jnp.int32, (tile, LANES), 0)
        lower = lax.broadcasted_iota(jnp.int32, (tile, LANES), 1) < HALF
        first = lax.broadcasted_iota(jnp.int32, (levels, LANES), 0) < half
        blank = jnp.zeros((levels, LANES - (share - LANES)), F32)

        for n, row in enumerate(rows):
            for part in range(parts):
                start = part * share
                main_ref[n, part] = row[:, start : start + LANES]
                rest = jnp.concatenate([row[:, start + LANES : start + share], blank], axis=1)
                rest_ref[n, part] = jnp.where(first, rest, roll(rest, HALF, 1))
        places = edge_rows(count)
        for low in range(0, count, tile):
            band = slice(low, low + tile)
            mine = [(n, place - low) for n, place in enumerate(places) if low <= place < low + tile]
            for part in range(parts):
                for l in range(levels):
                    value = sent_ref[part, l, band, :]
                    for n, place in mine:
                        value = jnp.where(sublane == place, main_ref[n, part, l : l + 1, :], value)
                    send_ref[part, l, band, :] = value
                for l in range(half):
                    value = sent_ref[part, levels + l, band, :]
                    for n, place in mine:
                        both = jnp.where(
                            lower, rest_ref[n, part, l : l + 1, :], rest_ref[n, part, l + half : l + half + 1, :]
                        )
                        value = jnp.where(sublane == place, both, value)
                    send_ref[part, levels + l, band, :] = value
    else:
        down_ref[0], down_ref[1] = rows[0][:, :lons], rows[1][:, :lons]
        up_ref[0], up_ref[1] = rows[3][:, :lons], rows[2][:, :lons]


def edges(below, above, edge, lonc, swept, *more):
    _, levels, lons = swept.shape
    final = len(more) > 0
    args = (below, above, edge, lonc, swept, *more)
    if final:
        out_shape = jax.ShapeDtypeStruct(more[-1].shape, F32)
        scratch = [pltpu.VMEM((4, more[-1].shape[0], levels, LANES), F32)] * 2
    else:
        out_shape = (jax.ShapeDtypeStruct((2, levels, lons), F32),) * 2
        scratch = []
    return pl.pallas_call(
        functools.partial(edges_kernel, final=final),
        out_shape=out_shape,
        in_specs=[VMEM] * len(args),
        out_specs=VMEM if final else (VMEM, VMEM),
        scratch_shapes=scratch,
        compiler_params=params(),
        cost_estimate=cost(1),
        name="edges",
    )(*args)


def pack_kernel(a_in, c_in, k_in, up_ref, down_ref, high_ref, low_ref, sems):
    edge = a_in.shape[1] - 1
    moves = (
        (k_in, edge, high_ref),
        (k_in, 0, low_ref),
        (a_in, edge, up_ref.at[0]),
        (a_in, edge - 1, up_ref.at[1]),
        (c_in, edge, up_ref.at[2]),
        (c_in, edge - 1, up_ref.at[3]),
        (a_in, 0, down_ref.at[0]),
        (a_in, 1, down_ref.at[1]),
        (c_in, 0, down_ref.at[2]),
    )
    copies = [pltpu.make_async_copy(src.at[:, row, :], dst, sems.at[n]) for n, (src, row, dst) in enumerate(moves)]
    for copy in copies:
        copy.start()
    for copy in copies:
        copy.wait()
    up_ref[4] = high_ref[...].astype(F32)
    down_ref[3] = low_ref[...].astype(F32)


def pack(a, clat, klat):
    levels, _, lons = a.shape
    row = (levels, lons)
    return pl.pallas_call(
        pack_kernel,
        out_shape=(jax.ShapeDtypeStruct((5, *row), F32), jax.ShapeDtypeStruct((4, *row), F32)),
        in_specs=[HBM] * 3,
        out_specs=(VMEM, VMEM),
        scratch_shapes=[pltpu.VMEM(row, klat.dtype)] * 2 + [pltpu.SemaphoreType.DMA((9,))],
        compiler_params=params(58),
        cost_estimate=cost(2),
        name="pack",
    )(a, clat, klat)


def prep_kernel(
    inverse_ref, lower_ref, upper_ref, owner_ref, ids_ref, matrix_ref, slot_ref, coarse_ref, fine_ref, device_ref, *, devices, parts
):
    lats, blocks, size, _ = inverse_ref.shape
    group = LANES // size
    levels = blocks * size
    row = lax.broadcasted_iota(jnp.int32, (LANES, LANES), 0)
    col = lax.broadcasted_iota(jnp.int32, (LANES, LANES), 1)
    diagonal = (row // size) == (col // size)
    row_l = lax.broadcasted_iota(jnp.int32, (LANES, levels), 0)
    col_l = lax.broadcasted_iota(jnp.int32, (LANES, levels), 1)

    def times(matrix, vector):
        wide = jnp.concatenate([matrix.reshape(LANES, size)] * group, axis=1)
        wide = jnp.where(diagonal, wide, 0.0)
        return jnp.dot(wide, vector, precision=lax.Precision.HIGHEST, preferred_element_type=F32)

    for first in range(0, lats, group):
        lat = slice(first, first + group)
        solved = []
        for k in range(blocks):
            rhs = jnp.where(col_l == row_l % size + size * k, 1.0, 0.0)
            if k > 0:
                rhs = rhs - times(lower_ref[lat, k - 1], solved[-1])
            solved.append(times(inverse_ref[lat, k], rhs))
        result = [solved[-1]]
        for k in range(blocks - 2, -1, -1):
            result.insert(0, solved[k] - times(upper_ref[lat, k], result[0]))
        for g in range(group):
            dense = jnp.concatenate([block[g * size : (g + 1) * size] for block in result], axis=0)
            high, low = split(dense.T)
            matrix_ref[first + g] = jnp.concatenate([high, low, high], axis=1)

    tiles = owner_ref.shape[0]
    device = lax.broadcasted_iota(jnp.int32, (devices, FINE), 0)
    row_f = lax.broadcasted_iota(jnp.int32, (FINE, FINE), 0)
    col_f = lax.broadcasted_iota(jnp.int32, (FINE, FINE), 1)
    earlier = jnp.where(row_f < col_f, 1.0, 0.0).astype(BF16)
    running = jnp.zeros((devices, 1), F32)
    for t in range(tiles):
        owned = jnp.where(owner_ref[pl.ds(t, 1), :] == device, 1.0, 0.0)
        before = jnp.dot(owned.astype(BF16), earlier, preferred_element_type=F32) + running
        slot_ref[pl.ds(t, 1), :] = jnp.sum(owned * before, axis=0, keepdims=True).astype(jnp.int32)
        running = running + jnp.sum(owned, axis=1, keepdims=True)
    ids = ids_ref[...]
    share = ids.shape[1] // parts
    gap = jnp.full((lats, HALF - (share - LANES)), -1, jnp.int32)
    pieces = [ids[:, part * share : part * share + LANES] for part in range(parts)]
    for part in range(parts):
        pieces += [ids[:, part * share + LANES : (part + 1) * share], gap]
    ids = jnp.concatenate(pieces, axis=1)
    coarse_ref[...] = (ids >> FINE_BITS).astype(F32)
    fine_ref[...] = (ids & (FINE - 1)).astype(F32).T
    device_ref[...] = owner_ref[...].astype(F32).T


def prep(inverse, lower, upper, owner_tiles, ids, devices, parts):
    lats, blocks, size, _ = inverse.shape
    width = parts * (LANES + HALF)
    levels = blocks * size
    return pl.pallas_call(
        functools.partial(prep_kernel, devices=devices, parts=parts),
        out_shape=(
            jax.ShapeDtypeStruct((lats, levels, 3 * levels), BF16),
            jax.ShapeDtypeStruct(owner_tiles.shape, jnp.int32),
            jax.ShapeDtypeStruct((lats, width), F32),
            jax.ShapeDtypeStruct((width, lats), F32),
            jax.ShapeDtypeStruct(owner_tiles.shape[::-1], F32),
        ),
        in_specs=[VMEM] * 5,
        out_specs=(VMEM,) * 5,
        compiler_params=params(60),
        cost_estimate=cost(5),
        name="prep",
    )(inverse, lower, upper, owner_tiles, ids)


def unpacked(main, rest, upper, spare):
    if upper:
        rest = roll(rest, HALF, rest.ndim - 1)
    return jnp.concatenate([main, rest[..., :spare]], axis=-1)


def column_rows(ref, part, lat, group, rows):
    half = group // 2
    first = part * (group + half) * rows + lat
    main = ref[pl.ds(first, group, stride=rows), :]
    return main, ref[pl.ds(first + group * rows, half, stride=rows), :]


def vertical_kernel(x_ref, matrix_ref, c_ref, k_ref, out_ref, main_ref, rest_ref, *, group):
    levels, rows, share = c_ref.shape
    half = group // 2
    parts = levels // group
    spare = share - LANES
    for lat in range(rows):
        mains, rests = [], []
        for part in range(parts):
            main, rest = column_rows(x_ref, part, lat, group, rows)
            mains.append(main)
            rests += [rest, roll(rest, HALF, 1)]
        x = jnp.concatenate([jnp.concatenate(mains, axis=0), jnp.concatenate(rests, axis=0)], axis=1)
        high, low = split(x)
        stacked = jnp.concatenate([high, high, low], axis=0)
        y = jnp.dot(matrix_ref[lat], stacked, preferred_element_type=F32)
        main_ref[pl.ds(lat, levels, stride=rows), :] = y[:, :LANES]
        rest_ref[pl.ds(lat, levels, stride=rows), :] = y[:, LANES:]

    def y_at(level):
        band = slice(level * rows, (level + 1) * rows)
        return jnp.concatenate([main_ref[band, :], rest_ref[band, :spare]], axis=1)

    def emit(level, value):
        part, l = level // group, level % group
        first = part * (group + half) * rows
        band = slice(first + l * rows, first + (l + 1) * rows)
        out_ref[band, :] = value[:, :LANES]
        place = first + (group + l % half) * rows
        side = l // half * HALF
        out_ref[place : place + rows, side : side + spare] = value[:, LANES:]

    zero = jnp.zeros((rows, share), F32)
    y = y_at(0)
    prior_w, prior_q, pending = zero, zero, None
    for i in range(levels):
        ahead, behind = slope_parts(k_ref[i])
        if i < levels - 1:
            up, down, uph, downh = flux_parts(c_ref[i])
            y_next = y_at(i + 1)
            f = y_next - y
            s = uph * f - prior_w
            here = y + up * f + prior_q
            prior_w = downh * f
            prior_q = down * f + ahead * s
        else:
            y_next = None
            s = -prior_w
            here = y + prior_q
        here = here + (behind - ahead) * s
        if i > 0:
            emit(i - 1, pending - behind * s)
        pending = here
        y = y_next
    emit(levels - 1, pending)


def vertical(x, matrix, courant, codes, group):
    levels, rows, _ = courant.shape
    return pl.pallas_call(
        functools.partial(vertical_kernel, group=group),
        out_shape=jax.ShapeDtypeStruct(x.shape, F32),
        in_specs=[VMEM] * 4,
        out_specs=VMEM,
        scratch_shapes=[pltpu.VMEM((levels * rows, LANES), F32)] * 2,
        compiler_params=params(),
        cost_estimate=cost(5),
        name="vertical",
    )(x, matrix, courant, codes)


def whole_row(field_ref, l, levels, lons):
    parts = field_ref.shape[0]
    half = levels // 2
    spare = lons // parts - LANES
    return jnp.concatenate(
        [unpacked(field_ref[p, l], field_ref[p, levels + l % half], l // half, spare) for p in range(parts)], axis=1
    )


def rejoin_kernel(field_ref, out_ref):
    levels, _, lons = out_ref.shape
    for l in range(levels):
        out_ref[l] = whole_row(field_ref, l, levels, lons)


def rejoin(field, shape):
    return pl.pallas_call(
        rejoin_kernel,
        out_shape=jax.ShapeDtypeStruct(shape, F32),
        in_specs=[VMEM],
        out_specs=VMEM,
        compiler_params=params(),
        cost_estimate=cost(2),
        name="rejoin",
    )(field)


def region_kernel(field_ref, coarse_ref, fine_ref, device_ref, slot_ref, send_ref, acc_ref, *, levels, scale):
    rows, width = coarse_ref.shape
    parts = width // (LANES + HALF)
    half = levels // 2
    tiles = slot_ref.shape[0]
    devices = send_ref.shape[0]
    lane = lax.broadcasted_iota(jnp.int32, (width, FINE), 1).astype(F32)
    lower = lax.broadcasted_iota(jnp.int32, (half, LANES), 1) < HALF
    for lat in range(rows):
        mains, rests = [], []
        for part in range(parts):
            main, rest = column_rows(field_ref, part, lat, levels, rows)
            mains.append(main)
            rests.append(rest)
        for even, odd in zip(rests[::2], rests[1::2]):
            first = jnp.where(lower, even, roll(odd, HALF, 1))
            second = jnp.where(lower, roll(even, HALF, 1), odd)
            mains.append(jnp.concatenate([first, second], axis=0))
        field = jnp.concatenate(mains, axis=1)
        high = field.astype(BF16).astype(F32)
        both = jnp.concatenate([high, field - high], axis=0)
        coarse = jnp.broadcast_to(coarse_ref[lat : lat + 1, :], both.shape)
        onehot = jnp.where(fine_ref[:, lat : lat + 1] == lane, 1.0, 0.0).astype(BF16)
        stacked = jnp.concatenate([jnp.where(coarse == t, both, 0.0).astype(BF16) for t in range(tiles)], axis=0)
        term = jnp.dot(stacked, onehot, preferred_element_type=F32)
        if lat == 0:
            acc_ref[...] = term
        else:
            acc_ref[...] += term
    device = lax.broadcasted_iota(jnp.int32, (FINE, devices), 1).astype(F32)
    place = lax.broadcasted_iota(jnp.int32, (SLOTS * levels, FINE), 0) // levels
    total = jnp.zeros((SLOTS * levels, devices), F32)
    for t in range(tiles):
        owned = jnp.where(device_ref[:, t : t + 1] == device, 1.0, 0.0).astype(BF16)
        base = 2 * levels * t
        sums = acc_ref[base : base + levels, :] + acc_ref[base + levels : base + 2 * levels, :]
        spread = jnp.where(slot_ref[t : t + 1, :] == place, jnp.concatenate([sums] * SLOTS, axis=0), 0.0)
        for piece in split(spread):
            total += jnp.dot(piece, owned, preferred_element_type=F32)
    send_ref[...] = (total * scale).T


def regions(field, coarse, fine, device, slot_tiles, levels, devices, scale):
    tiles = slot_tiles.shape[0]
    return pl.pallas_call(
        functools.partial(region_kernel, levels=levels, scale=scale),
        out_shape=jax.ShapeDtypeStruct((devices, SLOTS * levels), F32),
        in_specs=[VMEM] * 5,
        out_specs=VMEM,
        scratch_shapes=[pltpu.VMEM((2 * levels * tiles, FINE), F32)],
        compiler_params=params(),
        cost_estimate=cost(6),
        name="regions",
    )(field, coarse, fine, device, slot_tiles)


def owners_kernel(rows_ref, out_ref):
    devices, lanes = rows_ref.shape
    slots, width = out_ref.shape
    levels = lanes // slots
    groups = width // levels
    total = rows_ref[pl.ds(0, groups), :]
    for first in range(groups, devices, groups):
        total += rows_ref[pl.ds(first, groups), :]
    slot = lax.broadcasted_iota(jnp.int32, (slots, lanes), 0)
    lane = lax.broadcasted_iota(jnp.int32, (slots, lanes), 1)
    mine = slot == lane // levels
    spread = jnp.concatenate([jnp.where(mine, total[j : j + 1], 0.0) for j in range(groups)], axis=1)
    row = lax.broadcasted_iota(jnp.int32, (groups * lanes, width), 0)
    col = lax.broadcasted_iota(jnp.int32, (groups * lanes, width), 1)
    fold = jnp.where(col == row // lanes * levels + row % levels, 1.0, 0.0)
    out_ref[...] = jnp.dot(spread, fold, precision=lax.Precision.HIGHEST, preferred_element_type=F32)


def owners(rows, groups, levels):
    return pl.pallas_call(
        owners_kernel,
        out_shape=jax.ShapeDtypeStruct((SLOTS, groups * levels), F32),
        in_specs=[VMEM],
        out_specs=VMEM,
        compiler_params=params(),
        name="owners",
    )(rows)


def neighbours(up, down):
    count = lax.axis_size("lat")
    forward = [(i, i + 1) for i in range(count - 1)]
    backward = [(target, source) for source, target in forward]
    return lax.ppermute(up, "lat", forward), lax.ppermute(down, "lat", backward)


def local(
    adjoint_in,
    courant_lon,
    codes_lon,
    courant_lat,
    codes_lat,
    courant_lev,
    codes_lev,
    block_inverse,
    block_lower,
    block_upper,
    region_ids,
    owner,
):
    levels_here, bands_here, lon_cells = adjoint_in.shape
    band_count = lax.axis_size("lat")
    group_count = lax.axis_size("lev")
    devices = band_count * group_count
    region_count = owner.shape[0]
    tiles = -(-region_count // (8 * FINE)) * 8
    owner_tiles = jnp.pad(owner, (0, tiles * FINE - region_count), constant_values=-1).reshape(tiles, FINE)
    matrix, slot_tiles, coarse, fine, device = prep(
        block_inverse, block_lower, block_upper, owner_tiles, region_ids, devices, group_count
    )
    last = (lax.axis_index("lat") == band_count - 1).astype(jnp.int32).reshape(1)
    up, down = pack(adjoint_in, courant_lat, codes_lat)
    below, above = neighbours(up, down)
    coefficients = (courant_lat, codes_lat, courant_lon, codes_lon)
    partial, swept, edge = first_lat(last, adjoint_in, courant_lat, codes_lat)
    adjoint, lonc = first_lon(partial, courant_lon, codes_lon)
    up, down = edges(below, above, edge, lonc, swept)
    below_next, above_next = neighbours(up, down)
    sent, swept = interior(last, (adjoint, up, down), coefficients, group_count)
    sent = edges(below, above, edge, lonc, swept, below_next, above_next, up, down, sent)
    columns = lax.all_to_all(sent, "lev", split_axis=0, concat_axis=0, tiled=True)
    columns = vertical(columns.reshape(-1, LANES), matrix, courant_lev, codes_lev, levels_here)
    field = lax.all_to_all(columns.reshape(sent.shape), "lev", split_axis=0, concat_axis=0, tiled=True)
    scale = (region_count / (bands_here * band_count * lon_cells)) ** 0.5
    rows = regions(field.reshape(-1, LANES), coarse, fine, device, slot_tiles, levels_here, devices, scale)
    rows = lax.all_to_all(rows, ("lat", "lev"), split_axis=0, concat_axis=0, tiled=True)
    adjoint_out = rejoin(field, adjoint_in.shape)
    region_sens = owners(rows, group_count, levels_here)
    return (adjoint_out, region_sens)


def solution(mesh):
    placed = (
        P("lev", "lat", None),
        P("lev", "lat", None),
        P("lev", "lat", None),
        P("lev", "lat", None),
        P("lev", "lat", None),
        P(None, "lat", "lev"),
        P(None, "lat", "lev"),
        P("lat", None, None, None),
        P("lat", None, None, None),
        P("lat", None, None, None),
        P("lat", None),
        P(),
    )
    return jax.shard_map(
        local,
        mesh=mesh,
        in_specs=placed,
        out_specs=(P("lev", "lat", None), P(("lat", "lev"), None)),
        check_vma=False,
    )
```

```python
import functools

import jax
import jax.numpy as jnp
from jax import lax
from jax.experimental import pallas as pl
from jax.experimental.pallas import tpu as pltpu
from jax.sharding import PartitionSpec as P

SUB = 2
SLOTS = 16
LANES = 128
HALF = LANES // 2
FINE_BITS = 8
FINE = 2**FINE_BITS
F32 = jnp.float32
BF16 = jnp.bfloat16
VMEM = pl.BlockSpec(memory_space=pltpu.VMEM)
SMEM = pl.BlockSpec(memory_space=pltpu.SMEM)
HBM = pl.BlockSpec(memory_space=pltpu.HBM)


def params(mib=20):
    return pltpu.CompilerParams(vmem_limit_bytes=mib * 2**20)


def cost(microseconds):
    return pl.CostEstimate(flops=microseconds * 10**9, bytes_accessed=microseconds * 10**6, transcendentals=0)


def flux_parts(courant):
    up = jnp.maximum(courant, 0.0)
    down = jnp.minimum(courant, 0.0)
    half = 0.5 * courant
    return up, down, up * (0.5 - half), down * (0.5 + half)


def slope_parts(codes):
    centred = jnp.where(codes == 3, 0.5, 0.0)
    ahead = jnp.where(codes == 1, 1.0, centred)
    behind = jnp.where(codes == 2, 1.0, centred)
    return ahead, behind


def split(value):
    high = value.astype(BF16)
    low = (value - high.astype(F32)).astype(BF16)
    return high, low


def roll(value, shift, axis):
    return pltpu.roll(value, shift % value.shape[axis], axis)


def wrapped(value, width):
    length = value.shape[1]
    spare = width - length
    first = spare // 2
    return jnp.concatenate([value, value[:, :first], value[:, length - spare + first :]], axis=1)


def sweep_lon(value, up, down, uph, downh, ahead, behind):
    f = roll(value, -1, 1) - value
    s = uph * f - roll(downh * f, 1, 1)
    q = roll(down * f + ahead * s, 1, 1)
    r = roll(behind * s, -1, 1)
    return value + up * f + (behind - ahead) * s + q - r


def lon_parts(courant, codes, width):
    return (*flux_parts(wrapped(courant, width)), *slope_parts(wrapped(codes, width)))


def edge_rows(rows):
    return (0, 1, rows - 2, rows - 1)


def sweep_lat(a, courant, codes):
    rows, size = a.shape
    row = lax.broadcasted_iota(jnp.int32, (rows, size), 0)
    lowest, highest = row == 0, row == rows - 1
    up, down, uph, downh = flux_parts(courant)
    ahead, behind = slope_parts(codes)
    f = jnp.where(highest, 0.0, roll(a, -1, 0)) - a
    s = uph * f - jnp.where(lowest, 0.0, roll(downh * f, 1, 0))
    q = jnp.where(lowest, 0.0, roll(down * f + ahead * s, 1, 0))
    r = jnp.where(highest, 0.0, roll(behind * s, -1, 0))
    return a + up * f + (behind - ahead) * s + q - r


def lane_chunks(lons):
    step = 4 * LANES
    return [slice(start, min(start + step, lons)) for start in range(0, lons, step)]


def walled(last, courant):
    rows = courant.shape[0]
    row = lax.broadcasted_iota(jnp.int32, courant.shape, 0)
    return jnp.where((row == rows - 1) & (last == 1), 0.0, courant)


def first_lat_kernel(last_ref, a_ref, clat_ref, klat_ref, rows_ref, swept_ref, edge_ref):
    levels, rows, lons = a_ref.shape
    last = last_ref[0]

    def level(l, carry):
        for cols in lane_chunks(lons):
            rows_ref[l, :, cols] = sweep_lat(
                a_ref[l, :, cols], walled(last, clat_ref[l, :, cols]), klat_ref[l, :, cols]
            )
        return carry

    lax.fori_loop(0, levels, level, 0)
    for n, row in enumerate(edge_rows(rows)):
        swept_ref[n] = rows_ref[:, row, :]
    high = rows - 1
    courant = jnp.where(last == 1, 0.0, clat_ref[:, high, :])
    up, _, uph, downh = flux_parts(courant)
    ahead, behind = slope_parts(klat_ref[:, high, :])
    ahead0, behind0 = slope_parts(klat_ref[:, 0, :])
    edge_ref[0] = a_ref[:, 0, :]
    edge_ref[1] = a_ref[:, high, :]
    edge_ref[2] = behind0 - ahead0
    edge_ref[3] = ahead0
    edge_ref[4] = up + (behind - ahead) * uph
    edge_ref[5] = behind * uph
    edge_ref[6] = downh


def first_lat(last, a, clat, klat):
    levels, rows, lons = a.shape
    return pl.pallas_call(
        first_lat_kernel,
        out_shape=(
            jax.ShapeDtypeStruct(a.shape, F32),
            jax.ShapeDtypeStruct((4, levels, lons), F32),
            jax.ShapeDtypeStruct((7, levels, lons), F32),
        ),
        in_specs=[SMEM] + [VMEM] * 3,
        out_specs=(VMEM,) * 3,
        compiler_params=params(),
        cost_estimate=cost(2),
        name="first_lat",
    )(last, a, clat, klat)


def first_lon_kernel(rows_ref, clon_ref, klon_ref, out_ref, lonc_ref):
    levels, rows, lons = rows_ref.shape
    width = lonc_ref.shape[3]
    tile = 8

    def level(l, carry):
        for low in range(0, rows, tile):
            band = slice(low, low + tile)
            value = sweep_lon(
                wrapped(rows_ref[l, band, :], width), *lon_parts(clon_ref[l, band, :], klon_ref[l, band, :], width)
            )
            out_ref[l, band, :] = value[:, :lons]
        return carry

    lax.fori_loop(0, levels, level, 0)
    for n, row in enumerate(edge_rows(rows)):
        for m, part in enumerate(lon_parts(clon_ref[:, row, :], klon_ref[:, row, :], width)):
            lonc_ref[n, m] = part


def first_lon(swept, clon, klon):
    levels, _, lons = swept.shape
    width = -(-lons // LANES) * LANES
    return pl.pallas_call(
        first_lon_kernel,
        out_shape=(jax.ShapeDtypeStruct(swept.shape, F32), jax.ShapeDtypeStruct((4, 6, levels, width), F32)),
        in_specs=[VMEM] * 3,
        out_specs=(VMEM,) * 2,
        compiler_params=params(),
        cost_estimate=cost(2),
        name="first_lon",
    )(swept, clon, klon)


def interior_kernel(
    last_ref, a_ref, up_ref, down_ref, clat_ref, klat_ref, clon_ref, klon_ref, send_ref, swept_ref, rows_ref
):
    levels, rows, lons = a_ref.shape
    width = rows_ref.shape[2]
    half = levels // 2
    last = last_ref[0]
    tile = 8

    def level(l, upper):
        for cols in lane_chunks(lons):
            a = a_ref[l, :, cols]
            row = lax.broadcasted_iota(jnp.int32, a.shape, 0)
            a = jnp.where(row == 0, down_ref[0, pl.ds(l, 1), cols], a)
            a = jnp.where(row == 1, down_ref[1, pl.ds(l, 1), cols], a)
            a = jnp.where(row == rows - 2, up_ref[1, pl.ds(l, 1), cols], a)
            a = jnp.where(row == rows - 1, up_ref[0, pl.ds(l, 1), cols], a)
            rows_ref[l, :, cols] = sweep_lat(a, walled(last, clat_ref[l, :, cols]), klat_ref[l, :, cols])
        parts = send_ref.shape[0]
        share = lons // parts
        for low in range(0, rows, tile):
            band = slice(low, low + tile)
            value = sweep_lon(
                wrapped(rows_ref[l, band, :lons], width), *lon_parts(clon_ref[l, band, :], klon_ref[l, band, :], width)
            )
            for part in range(parts):
                start = part * share
                send_ref[part, l, band, :] = value[:, start : start + LANES]
                rest = value[:, start + LANES : start + share]
                if upper:
                    send_ref[part, half + l, band, HALF : HALF + share - LANES] = rest
                else:
                    send_ref[part, levels + l, band, : share - LANES] = rest

    def pair(index, carry):
        level(index, False)
        level(index + half, True)
        return carry

    lax.fori_loop(0, half, pair, 0)
    for n, row in enumerate(edge_rows(rows)):
        swept_ref[n] = rows_ref[:, row, :lons]


def interior(last, fields, coefficients, parts):
    levels, rows, lons = fields[0].shape
    width = -(-lons // LANES) * LANES
    return pl.pallas_call(
        interior_kernel,
        out_shape=(
            jax.ShapeDtypeStruct((parts, levels + levels // 2, rows, LANES), F32),
            jax.ShapeDtypeStruct((4, levels, lons), F32),
        ),
        in_specs=[SMEM] + [VMEM] * (len(fields) + len(coefficients)),
        out_specs=(VMEM,) * 2,
        scratch_shapes=[pltpu.VMEM((levels, rows, width), F32)],
        compiler_params=params(),
        cost_estimate=cost(4),
        name="interior",
    )(last, *fields, *coefficients)


def edges_kernel(below_ref, above_ref, edge_ref, lonc_ref, swept_ref, *refs, final):
    width = lonc_ref.shape[3]
    _, levels, lons = swept_ref.shape
    if final:
        below_next, above_next, up_in, down_in, sent_ref, send_ref, main_ref, rest_ref = refs
        row0, row15 = down_in[0], up_in[0]
        am1, am2, a16, a17 = below_next[0], below_next[1], above_next[0], above_next[1]
    else:
        up_ref, down_ref = refs
        row0, row15 = edge_ref[0], edge_ref[1]
        am1, am2, a16, a17 = below_ref[0], below_ref[1], above_ref[0], above_ref[1]
    _, down1, uph1, downh1 = flux_parts(below_ref[2])
    _, _, _, downh2 = flux_parts(below_ref[3])
    ahead1, _ = slope_parts(below_ref[4])
    f1 = row0 - am1
    w = downh1 * f1
    q = down1 * f1 + ahead1 * (uph1 * f1 - downh2 * (am1 - am2))
    _, _, uph16, _ = flux_parts(above_ref[2])
    _, behind16 = slope_parts(above_ref[3])
    r = behind16 * (uph16 * (a17 - a16) - edge_ref[6] * (a16 - row15))
    fixed = (
        swept_ref[0] - edge_ref[2] * w + q,
        swept_ref[1] - edge_ref[3] * w,
        swept_ref[2] - edge_ref[5] * a16,
        swept_ref[3] + edge_ref[4] * a16 - r,
    )
    rows = []
    for n, row in enumerate(fixed):
        rows.append(sweep_lon(wrapped(row, width), *(lonc_ref[n, m] for m in range(6))))
    if final:
        parts, _, count, _ = send_ref.shape
        share = lons // parts
        half = levels // 2
        tile = 8
        sublane = lax.broadcasted_iota(jnp.int32, (tile, LANES), 0)
        lower = lax.broadcasted_iota(jnp.int32, (tile, LANES), 1) < HALF
        first = lax.broadcasted_iota(jnp.int32, (levels, LANES), 0) < half
        blank = jnp.zeros((levels, LANES - (share - LANES)), F32)

        for n, row in enumerate(rows):
            for part in range(parts):
                start = part * share
                main_ref[n, part] = row[:, start : start + LANES]
                rest = jnp.concatenate([row[:, start + LANES : start + share], blank], axis=1)
                rest_ref[n, part] = jnp.where(first, rest, roll(rest, HALF, 1))
        places = edge_rows(count)
        for low in range(0, count, tile):
            band = slice(low, low + tile)
            mine = [(n, place - low) for n, place in enumerate(places) if low <= place < low + tile]
            for part in range(parts):
                for l in range(levels):
                    value = sent_ref[part, l, band, :]
                    for n, place in mine:
                        value = jnp.where(sublane == place, main_ref[n, part, l : l + 1, :], value)
                    send_ref[part, l, band, :] = value
                for l in range(half):
                    value = sent_ref[part, levels + l, band, :]
                    for n, place in mine:
                        both = jnp.where(
                            lower, rest_ref[n, part, l : l + 1, :], rest_ref[n, part, l + half : l + half + 1, :]
                        )
                        value = jnp.where(sublane == place, both, value)
                    send_ref[part, levels + l, band, :] = value
    else:
        down_ref[0], down_ref[1] = rows[0][:, :lons], rows[1][:, :lons]
        up_ref[0], up_ref[1] = rows[3][:, :lons], rows[2][:, :lons]


def edges(below, above, edge, lonc, swept, *more):
    _, levels, lons = swept.shape
    final = len(more) > 0
    args = (below, above, edge, lonc, swept, *more)
    if final:
        out_shape = jax.ShapeDtypeStruct(more[-1].shape, F32)
        scratch = [pltpu.VMEM((4, more[-1].shape[0], levels, LANES), F32)] * 2
    else:
        out_shape = (jax.ShapeDtypeStruct((2, levels, lons), F32),) * 2
        scratch = []
    return pl.pallas_call(
        functools.partial(edges_kernel, final=final),
        out_shape=out_shape,
        in_specs=[VMEM] * len(args),
        out_specs=VMEM if final else (VMEM, VMEM),
        scratch_shapes=scratch,
        compiler_params=params(),
        cost_estimate=cost(1),
        name="edges",
    )(*args)


def pack_kernel(a_in, c_in, k_in, up_ref, down_ref, high_ref, low_ref, sems):
    edge = a_in.shape[1] - 1
    moves = (
        (k_in, edge, high_ref),
        (k_in, 0, low_ref),
        (a_in, edge, up_ref.at[0]),
        (a_in, edge - 1, up_ref.at[1]),
        (c_in, edge, up_ref.at[2]),
        (c_in, edge - 1, up_ref.at[3]),
        (a_in, 0, down_ref.at[0]),
        (a_in, 1, down_ref.at[1]),
        (c_in, 0, down_ref.at[2]),
    )
    copies = [pltpu.make_async_copy(src.at[:, row, :], dst, sems.at[n]) for n, (src, row, dst) in enumerate(moves)]
    for copy in copies:
        copy.start()
    for copy in copies:
        copy.wait()
    up_ref[4] = high_ref[...].astype(F32)
    down_ref[3] = low_ref[...].astype(F32)


def pack(a, clat, klat):
    levels, _, lons = a.shape
    row = (levels, lons)
    return pl.pallas_call(
        pack_kernel,
        out_shape=(jax.ShapeDtypeStruct((5, *row), F32), jax.ShapeDtypeStruct((4, *row), F32)),
        in_specs=[HBM] * 3,
        out_specs=(VMEM, VMEM),
        scratch_shapes=[pltpu.VMEM(row, klat.dtype)] * 2 + [pltpu.SemaphoreType.DMA((9,))],
        compiler_params=params(58),
        cost_estimate=cost(2),
        name="pack",
    )(a, clat, klat)


def prep_kernel(
    inverse_ref, lower_ref, upper_ref, owner_ref, ids_ref, matrix_ref, slot_ref, coarse_ref, fine_ref, device_ref, *, devices, parts
):
    lats, blocks, size, _ = inverse_ref.shape
    group = LANES // size
    levels = blocks * size
    row = lax.broadcasted_iota(jnp.int32, (LANES, LANES), 0)
    col = lax.broadcasted_iota(jnp.int32, (LANES, LANES), 1)
    diagonal = (row // size) == (col // size)
    row_l = lax.broadcasted_iota(jnp.int32, (LANES, levels), 0)
    col_l = lax.broadcasted_iota(jnp.int32, (LANES, levels), 1)

    def times(matrix, vector):
        wide = jnp.concatenate([matrix.reshape(LANES, size)] * group, axis=1)
        wide = jnp.where(diagonal, wide, 0.0)
        return jnp.dot(wide, vector, precision=lax.Precision.HIGHEST, preferred_element_type=F32)

    for first in range(0, lats, group):
        lat = slice(first, first + group)
        solved = []
        for k in range(blocks):
            rhs = jnp.where(col_l == row_l % size + size * k, 1.0, 0.0)
            if k > 0:
                rhs = rhs - times(lower_ref[lat, k - 1], solved[-1])
            solved.append(times(inverse_ref[lat, k], rhs))
        result = [solved[-1]]
        for k in range(blocks - 2, -1, -1):
            result.insert(0, solved[k] - times(upper_ref[lat, k], result[0]))
        for g in range(group):
            dense = jnp.concatenate([block[g * size : (g + 1) * size] for block in result], axis=0)
            high, low = split(dense.T)
            matrix_ref[first + g] = jnp.concatenate([high, low, high], axis=1)

    tiles = owner_ref.shape[0]
    device = lax.broadcasted_iota(jnp.int32, (devices, FINE), 0)
    row_f = lax.broadcasted_iota(jnp.int32, (FINE, FINE), 0)
    col_f = lax.broadcasted_iota(jnp.int32, (FINE, FINE), 1)
    earlier = jnp.where(row_f < col_f, 1.0, 0.0).astype(BF16)
    running = jnp.zeros((devices, 1), F32)
    for t in range(tiles):
        owned = jnp.where(owner_ref[pl.ds(t, 1), :] == device, 1.0, 0.0)
        before = jnp.dot(owned.astype(BF16), earlier, preferred_element_type=F32) + running
        slot_ref[pl.ds(t, 1), :] = jnp.sum(owned * before, axis=0, keepdims=True).astype(jnp.int32)
        running = running + jnp.sum(owned, axis=1, keepdims=True)
    ids = ids_ref[...]
    share = ids.shape[1] // parts
    gap = jnp.full((lats, HALF - (share - LANES)), -1, jnp.int32)
    pieces = [ids[:, part * share : part * share + LANES] for part in range(parts)]
    for part in range(parts):
        pieces += [ids[:, part * share + LANES : (part + 1) * share], gap]
    ids = jnp.concatenate(pieces, axis=1)
    coarse_ref[...] = (ids >> FINE_BITS).astype(F32)
    fine_ref[...] = (ids & (FINE - 1)).astype(F32).T
    device_ref[...] = owner_ref[...].astype(F32).T


def prep(inverse, lower, upper, owner_tiles, ids, devices, parts):
    lats, blocks, size, _ = inverse.shape
    width = parts * (LANES + HALF)
    levels = blocks * size
    return pl.pallas_call(
        functools.partial(prep_kernel, devices=devices, parts=parts),
        out_shape=(
            jax.ShapeDtypeStruct((lats, levels, 3 * levels), BF16),
            jax.ShapeDtypeStruct(owner_tiles.shape, jnp.int32),
            jax.ShapeDtypeStruct((lats, width), F32),
            jax.ShapeDtypeStruct((width, lats), F32),
            jax.ShapeDtypeStruct(owner_tiles.shape[::-1], F32),
        ),
        in_specs=[VMEM] * 5,
        out_specs=(VMEM,) * 5,
        compiler_params=params(60),
        cost_estimate=cost(5),
        name="prep",
    )(inverse, lower, upper, owner_tiles, ids)


def unpacked(main, rest, upper, spare):
    if upper:
        rest = roll(rest, HALF, rest.ndim - 1)
    return jnp.concatenate([main, rest[..., :spare]], axis=-1)


def column_rows(ref, part, lat, group, rows):
    half = group // 2
    first = part * (group + half) * rows + lat
    main = ref[pl.ds(first, group, stride=rows), :]
    return main, ref[pl.ds(first + group * rows, half, stride=rows), :]


def vertical_kernel(x_ref, matrix_ref, c_ref, k_ref, out_ref, main_ref, rest_ref, *, group):
    levels, rows, share = c_ref.shape
    half = group // 2
    parts = levels // group
    spare = share - LANES
    for lat in range(rows):
        mains, rests = [], []
        for part in range(parts):
            main, rest = column_rows(x_ref, part, lat, group, rows)
            mains.append(main)
            rests += [rest, roll(rest, HALF, 1)]
        x = jnp.concatenate([jnp.concatenate(mains, axis=0), jnp.concatenate(rests, axis=0)], axis=1)
        high, low = split(x)
        stacked = jnp.concatenate([high, high, low], axis=0)
        y = jnp.dot(matrix_ref[lat], stacked, preferred_element_type=F32)
        main_ref[pl.ds(lat, levels, stride=rows), :] = y[:, :LANES]
        rest_ref[pl.ds(lat, levels, stride=rows), :] = y[:, LANES:]

    def y_at(level):
        band = slice(level * rows, (level + 1) * rows)
        return jnp.concatenate([main_ref[band, :], rest_ref[band, :spare]], axis=1)

    def emit(level, value):
        part, l = level // group, level % group
        first = part * (group + half) * rows
        band = slice(first + l * rows, first + (l + 1) * rows)
        out_ref[band, :] = value[:, :LANES]
        place = first + (group + l % half) * rows
        side = l // half * HALF
        out_ref[place : place + rows, side : side + spare] = value[:, LANES:]

    zero = jnp.zeros((rows, share), F32)
    y = y_at(0)
    prior_w, prior_q, pending = zero, zero, None
    for i in range(levels):
        ahead, behind = slope_parts(k_ref[i])
        if i < levels - 1:
            up, down, uph, downh = flux_parts(c_ref[i])
            y_next = y_at(i + 1)
            f = y_next - y
            s = uph * f - prior_w
            here = y + up * f + prior_q
            prior_w = downh * f
            prior_q = down * f + ahead * s
        else:
            y_next = None
            s = -prior_w
            here = y + prior_q
        here = here + (behind - ahead) * s
        if i > 0:
            emit(i - 1, pending - behind * s)
        pending = here
        y = y_next
    emit(levels - 1, pending)


def vertical(x, matrix, courant, codes, group):
    levels, rows, _ = courant.shape
    return pl.pallas_call(
        functools.partial(vertical_kernel, group=group),
        out_shape=jax.ShapeDtypeStruct(x.shape, F32),
        in_specs=[VMEM] * 4,
        out_specs=VMEM,
        scratch_shapes=[pltpu.VMEM((levels * rows, LANES), F32)] * 2,
        compiler_params=params(),
        cost_estimate=cost(5),
        name="vertical",
    )(x, matrix, courant, codes)


def whole_row(field_ref, l, levels, lons):
    parts = field_ref.shape[0]
    half = levels // 2
    spare = lons // parts - LANES
    return jnp.concatenate(
        [unpacked(field_ref[p, l], field_ref[p, levels + l % half], l // half, spare) for p in range(parts)], axis=1
    )


def rejoin_kernel(field_ref, out_ref):
    levels, _, lons = out_ref.shape
    for l in range(levels):
        out_ref[l] = whole_row(field_ref, l, levels, lons)


def rejoin(field, shape):
    return pl.pallas_call(
        rejoin_kernel,
        out_shape=jax.ShapeDtypeStruct(shape, F32),
        in_specs=[VMEM],
        out_specs=VMEM,
        compiler_params=params(),
        cost_estimate=cost(2),
        name="rejoin",
    )(field)


def region_kernel(field_ref, coarse_ref, fine_ref, device_ref, slot_ref, send_ref, acc_ref, *, levels, scale):
    rows, width = coarse_ref.shape
    parts = width // (LANES + HALF)
    half = levels // 2
    tiles = slot_ref.shape[0]
    devices = send_ref.shape[0]
    lane = lax.broadcasted_iota(jnp.int32, (width, FINE), 1).astype(F32)
    lower = lax.broadcasted_iota(jnp.int32, (half, LANES), 1) < HALF
    for lat in range(rows):
        mains, rests = [], []
        for part in range(parts):
            main, rest = column_rows(field_ref, part, lat, levels, rows)
            mains.append(main)
            rests.append(rest)
        for even, odd in zip(rests[::2], rests[1::2]):
            first = jnp.where(lower, even, roll(odd, HALF, 1))
            second = jnp.where(lower, roll(even, HALF, 1), odd)
            mains.append(jnp.concatenate([first, second], axis=0))
        field = jnp.concatenate(mains, axis=1)
        high = field.astype(BF16).astype(F32)
        both = jnp.concatenate([high, field - high], axis=0)
        coarse = jnp.broadcast_to(coarse_ref[lat : lat + 1, :], both.shape)
        onehot = jnp.where(fine_ref[:, lat : lat + 1] == lane, 1.0, 0.0).astype(BF16)
        stacked = jnp.concatenate([jnp.where(coarse == t, both, 0.0).astype(BF16) for t in range(tiles)], axis=0)
        term = jnp.dot(stacked, onehot, preferred_element_type=F32)
        if lat == 0:
            acc_ref[...] = term
        else:
            acc_ref[...] += term
    device = lax.broadcasted_iota(jnp.int32, (FINE, devices), 1).astype(F32)
    place = lax.broadcasted_iota(jnp.int32, (SLOTS * levels, FINE), 0) // levels
    total = jnp.zeros((SLOTS * levels, devices), F32)
    for t in range(tiles):
        owned = jnp.where(device_ref[:, t : t + 1] == device, 1.0, 0.0).astype(BF16)
        base = 2 * levels * t
        sums = acc_ref[base : base + levels, :] + acc_ref[base + levels : base + 2 * levels, :]
        spread = jnp.where(slot_ref[t : t + 1, :] == place, jnp.concatenate([sums] * SLOTS, axis=0), 0.0)
        for piece in split(spread):
            total += jnp.dot(piece, owned, preferred_element_type=F32)
    send_ref[...] = (total * scale).T


def regions(field, coarse, fine, device, slot_tiles, levels, devices, scale):
    tiles = slot_tiles.shape[0]
    return pl.pallas_call(
        functools.partial(region_kernel, levels=levels, scale=scale),
        out_shape=jax.ShapeDtypeStruct((devices, SLOTS * levels), F32),
        in_specs=[VMEM] * 5,
        out_specs=VMEM,
        scratch_shapes=[pltpu.VMEM((2 * levels * tiles, FINE), F32)],
        compiler_params=params(),
        cost_estimate=cost(6),
        name="regions",
    )(field, coarse, fine, device, slot_tiles)


def owners_kernel(rows_ref, out_ref):
    devices, lanes = rows_ref.shape
    slots, width = out_ref.shape
    levels = lanes // slots
    groups = width // levels
    total = rows_ref[pl.ds(0, groups), :]
    for first in range(groups, devices, groups):
        total += rows_ref[pl.ds(first, groups), :]
    slot = lax.broadcasted_iota(jnp.int32, (slots, lanes), 0)
    lane = lax.broadcasted_iota(jnp.int32, (slots, lanes), 1)
    mine = slot == lane // levels
    spread = jnp.concatenate([jnp.where(mine, total[j : j + 1], 0.0) for j in range(groups)], axis=1)
    row = lax.broadcasted_iota(jnp.int32, (groups * lanes, width), 0)
    col = lax.broadcasted_iota(jnp.int32, (groups * lanes, width), 1)
    fold = jnp.where(col == row // lanes * levels + row % levels, 1.0, 0.0).astype(BF16)
    high, low = split(spread)
    out_ref[...] = jnp.dot(high, fold, preferred_element_type=F32) + jnp.dot(low, fold, preferred_element_type=F32)


def owners(rows, groups, levels):
    return pl.pallas_call(
        owners_kernel,
        out_shape=jax.ShapeDtypeStruct((SLOTS, groups * levels), F32),
        in_specs=[VMEM],
        out_specs=VMEM,
        compiler_params=params(),
        name="owners",
    )(rows)


def neighbours(up, down):
    count = lax.axis_size("lat")
    forward = [(i, i + 1) for i in range(count - 1)]
    backward = [(target, source) for source, target in forward]
    return lax.ppermute(up, "lat", forward), lax.ppermute(down, "lat", backward)


def local(
    adjoint_in,
    courant_lon,
    codes_lon,
    courant_lat,
    codes_lat,
    courant_lev,
    codes_lev,
    block_inverse,
    block_lower,
    block_upper,
    region_ids,
    owner,
):
    levels_here, bands_here, lon_cells = adjoint_in.shape
    band_count = lax.axis_size("lat")
    group_count = lax.axis_size("lev")
    devices = band_count * group_count
    region_count = owner.shape[0]
    tiles = -(-region_count // (8 * FINE)) * 8
    owner_tiles = jnp.pad(owner, (0, tiles * FINE - region_count), constant_values=-1).reshape(tiles, FINE)
    matrix, slot_tiles, coarse, fine, device = prep(
        block_inverse, block_lower, block_upper, owner_tiles, region_ids, devices, group_count
    )
    last = (lax.axis_index("lat") == band_count - 1).astype(jnp.int32).reshape(1)
    up, down = pack(adjoint_in, courant_lat, codes_lat)
    below, above = neighbours(up, down)
    coefficients = (courant_lat, codes_lat, courant_lon, codes_lon)
    partial, swept, edge = first_lat(last, adjoint_in, courant_lat, codes_lat)
    adjoint, lonc = first_lon(partial, courant_lon, codes_lon)
    up, down = edges(below, above, edge, lonc, swept)
    below_next, above_next = neighbours(up, down)
    sent, swept = interior(last, (adjoint, up, down), coefficients, group_count)
    sent = edges(below, above, edge, lonc, swept, below_next, above_next, up, down, sent)
    columns = lax.all_to_all(sent, "lev", split_axis=0, concat_axis=0, tiled=True)
    columns = vertical(columns.reshape(-1, LANES), matrix, courant_lev, codes_lev, levels_here)
    field = lax.all_to_all(columns.reshape(sent.shape), "lev", split_axis=0, concat_axis=0, tiled=True)
    scale = (region_count / (bands_here * band_count * lon_cells)) ** 0.5
    rows = regions(field.reshape(-1, LANES), coarse, fine, device, slot_tiles, levels_here, devices, scale)
    rows = lax.all_to_all(rows, ("lat", "lev"), split_axis=0, concat_axis=0, tiled=True)
    adjoint_out = rejoin(field, adjoint_in.shape)
    region_sens = owners(rows, group_count, levels_here)
    return (adjoint_out, region_sens)


def solution(mesh):
    placed = (
        P("lev", "lat", None),
        P("lev", "lat", None),
        P("lev", "lat", None),
        P("lev", "lat", None),
        P("lev", "lat", None),
        P(None, "lat", "lev"),
        P(None, "lat", "lev"),
        P("lat", None, None, None),
        P("lat", None, None, None),
        P("lat", None, None, None),
        P("lat", None),
        P(),
    )
    return jax.shard_map(
        local,
        mesh=mesh,
        in_specs=placed,
        out_specs=(P("lev", "lat", None), P(("lat", "lev"), None)),
        check_vma=False,
    )
```
